256 devices in a mesh: dp: 8 (over x_lo, y), ctx: 32 (over x_hi, z, core).
Axes of the slice: x: 4 (x_hi: 2, x_lo: 2; x = x_hi * 2 + x_lo), y: 4, z: 8, core: 2. Of those that a mesh axis runs over, the one named last changes fastest.
Arguments:
- signal: bfloat16 [8, 256, 16384], P('dp', None, 'ctx'), may hold values from -6 to 6
- grad_out: bfloat16 [8, 256, 16384], P('dp', None, 'ctx'), may hold values from -6 to 6
- residue: float32 [16, 16], replicated, may hold values from -1.5 to 1.5
- decay: float32 [16, 16], replicated, may hold values from 3.0517578e-05 to 0.05
Outputs:
- grad_signal: bfloat16 [8, 256, 16384], P('dp', None, 'ctx')
- grad_residue: float32 [16, 16], replicated
- decay_projection: float32 [16, 16], replicated
The draws below stay inside these ranges and needn't reach their ends.
All inputs are finite; a program needn't handle non-finite values.
Results may differ from the reference program's by a relative error of at most 0.00105.
Values may be sent and summed in bfloat16 or wider, within the bound.
A program may use at most 64 MiB of HBM per device.

```python
import math
import jax
import jax.numpy as jnp
from jax import lax

GROUPS = 16
GROUP_CH = 16
MODES = 16
CHANNELS = 256
TOKENS = 16384
BATCH = 8


def block_scale(stream_key, shape, cuts, smallest, top_value):
    level = 1.0
    for position, shards_of in cuts:
        steps = jax.random.uniform(jax.random.fold_in(jax.random.fold_in(stream_key, 6), position), (shards_of,), jnp.float32, smallest / len(cuts), top_value / len(cuts))
        level = level * jnp.repeat(jnp.exp(steps), shape[position] // shards_of).reshape((-1,) + (1,) * (len(shape) - 1 - position))
    return level


def gaussian(key, shape, scale, reach, shards=(), dtype=jnp.bfloat16):
    loudness = block_scale(key, shape, shards, -0.22, 0.18) if shards else 1.0
    drawn = jax.random.normal(key, shape, jnp.float32) * scale * loudness
    return jnp.minimum(jnp.maximum(drawn, -reach), reach).astype(dtype)


def setup_inputs(seed: int = 0) -> dict:
    key_of = jax.random.split(jax.random.key(seed), 5)
    signal = gaussian(key_of[0], (BATCH, CHANNELS, TOKENS), 1.0, 6.0, ((0, 8), (2, 32)))
    grad_out = gaussian(key_of[1], (BATCH, CHANNELS, TOKENS), 1.0, 6.0, ((0, 8), (2, 32)))
    residue = gaussian(key_of[2], (GROUPS, MODES), 0.25, 1.5, (), jnp.float32)
    decay = jnp.clip(jnp.exp(jax.random.uniform(key_of[3], (GROUPS, MODES), jnp.float32, math.log(3.0517578125e-05), math.log(0.05))), 3.0517578125e-05, 0.05)
    return {"signal": signal, "grad_out": grad_out, "residue": residue, "decay": decay}


def mode_basis(decay, positions):
    norm = jnp.sqrt(-jnp.expm1(-2.0 * decay))
    return jnp.exp(-decay[:, :, None] * positions[None, None, :]) * norm[:, :, None]

def reference(signal, grad_out, residue, decay):
    positions = jnp.arange(TOKENS).astype(jnp.float32)
    basis = mode_basis(decay, positions)
    filt = jnp.einsum('gm,gms->gs', residue, basis, precision=lax.Precision.HIGHEST)
    filt = jnp.repeat(filt, GROUP_CH, axis=0)
    length = 2 * TOKENS
    spec_x = jnp.fft.rfft(signal.astype(jnp.float32), n=length, axis=-1)
    spec_g = jnp.fft.rfft(grad_out.astype(jnp.float32), n=length, axis=-1)
    spec_h = jnp.fft.rfft(filt, n=length, axis=-1)
    spectrum = lax.optimization_barrier(jnp.sum(spec_g * jnp.conj(spec_x), axis=0))
    filter_grad = jnp.fft.irfft(spectrum, n=length, axis=-1)[:, :TOKENS]
    grad_signal = jnp.fft.irfft(spec_g * jnp.conj(spec_h)[None], n=length, axis=-1)[..., :TOKENS]
    group_grad = lax.optimization_barrier(jnp.sum(filter_grad.reshape(GROUPS, GROUP_CH, TOKENS), axis=1))
    scale = 1.0 / math.sqrt(GROUP_CH * BATCH * TOKENS)
    grad_residue = jnp.einsum('gs,gms->gm', group_grad, basis, precision=lax.Precision.HIGHEST) * scale
    weighted = basis * decay[:, :, None] * positions[None, None, :]
    decay_projection = jnp.einsum('gs,gms->gm', group_grad, weighted, precision=lax.Precision.HIGHEST) * scale
    return (grad_signal.astype(jnp.bfloat16), grad_residue, decay_projection)
```

```python
import functools
import math

import jax
import jax.numpy as jnp
from jax import lax
from jax.experimental import pallas as pl
from jax.experimental.pallas import tpu as pltpu
from jax.sharding import PartitionSpec as P

MESH = pl.DeviceIdType.MESH
F32 = jnp.float32
BF16 = jnp.bfloat16
LANES = 128
HIGH = lax.Precision.HIGHEST


def iota(shape, dim):
    return lax.broadcasted_iota(jnp.int32, shape, dim)


def split(value):
    top = value.astype(BF16)
    return top, (value - top.astype(F32)).astype(BF16)


def wrap(value, size):
    return jnp.where(value >= size, value - size, value)


def down(value, rows):
    return jnp.concatenate([value[rows:], jnp.zeros((rows, value.shape[1]), value.dtype)], axis=0)


def nt(left, right):
    return lax.dot_general(left, right, (((1,), (1,)), ((), ())), preferred_element_type=F32)


def tn(left, right):
    return lax.dot_general(left, right, (((0,), (0,)), ((), ())), preferred_element_type=F32)


def nn(left, right):
    return jnp.dot(left, right, preferred_element_type=F32)


def all_wait(ref, sem):
    pltpu.make_async_copy(ref, ref, sem).wait()


def kernel(
    dims, x_hbm, g_hbm, res_hbm, dec_hbm, out_hbm, p_hbm, q_hbm,
    xv, gv, resv, decv, dcol, rcol, lg, lx, fwd, bwd, yg, yx, wout, hrow, xrev, lagv, outl, rx, outv, pv, qv,
    send1, recv1, sendl, recvl, send2, recv2, send3, recv3,
    in_sem, out_sem, s1, r1, sl, rl, s2, r2, s3, r3,
):
    parts, batch, groups, modes, per_group, width, scale = dims
    rows = groups * modes
    chunks = width // LANES
    me = lax.axis_index("ctx")
    row_of = lax.axis_index("dp")

    loads = []
    for i, (src, dst) in enumerate(
        ((dec_hbm, decv), (res_hbm, resv), (g_hbm.at[0], gv), (x_hbm.at[0], xv))
    ):
        loads.append(pltpu.make_async_copy(src, dst, in_sem.at[i]))
        loads[-1].start()
    barrier = pltpu.get_barrier_semaphore()
    for i in range(1, parts):
        pl.semaphore_signal(barrier, inc=1, device_id={"ctx": wrap(me + i, parts)}, device_id_type=MESH)
    for i in range(1, batch):
        pl.semaphore_signal(barrier, inc=1, device_id={"dp": wrap(row_of + i, batch)}, device_id_type=MESH)

    loads[0].wait()
    loads[1].wait()
    dec = decv[...]
    series = dec * dec
    series = 1.0 + series / 6.0 * (1.0 + series / 20.0 * (1.0 + series / 42.0 * (1.0 + series / 72.0)))
    norm = jnp.sqrt(2.0 * jnp.exp(-dec) * dec * series)
    eye = iota((modes, modes), 0) == iota((modes, modes), 1)
    for g in range(groups):
        at = slice(g * modes, (g + 1) * modes)
        for src, dst in ((dec, dcol), (resv[...] * norm, rcol)):
            column = jnp.sum(jnp.where(eye, src[g : g + 1, :], 0.0), axis=1, keepdims=True)
            dst[at, :] = jnp.broadcast_to(column, (modes, LANES))

    lane_pos = iota((modes, width), 1).astype(F32)
    back_pos = width - lane_pos
    for g in range(groups):
        at = slice(g * modes, (g + 1) * modes)
        second = slice(rows + g * modes, rows + (g + 1) * modes)
        d = jnp.concatenate([dcol[at, :]] * chunks, axis=1)
        for pos, keep, dst in ((lane_pos, fwd, lg), (back_pos, bwd, lx)):
            e = jnp.exp(-(d * pos))
            keep[at, :] = e
            dst[at, :width], dst[at, width:] = split(e)
            dst[second, :width], dst[second, width:] = split(e * pos)

    loads[2].wait()
    yg[...] = nt(lg[...], jnp.concatenate([gv[...], gv[...]], axis=1))
    loads[3].wait()
    yx[...] = nt(lx[...], jnp.concatenate([xv[...], xv[...]], axis=1))

    segment = iota((8, LANES), 1) // per_group
    own_segment = segment == iota((8, LANES), 0)
    turned_segment = [segment == (iota((8, LANES), 0) + seg) % 8 for seg in range(8)]
    for k in range(parts):
        first = (k * 8 // modes) * per_group
        half, seg = first // LANES, (first % LANES) // per_group
        for kind, src in enumerate((yg, yg, yx, yx)):
            r0 = (kind % 2) * rows + k * 8
            v = src[r0 : r0 + 8, half * LANES : (half + 1) * LANES]
            v = pltpu.roll(v, 0, axis=1, stride=per_group, stride_axis=0)
            send1[k, kind : kind + 1, :] = jnp.sum(jnp.where(turned_segment[seg], v, 0.0), axis=0, keepdims=True)

    pl.semaphore_wait(barrier, parts - 1 + batch - 1)
    for i in range(1, parts):
        to = wrap(me + i, parts)
        pltpu.make_async_remote_copy(
            src_ref=send1.at[to], dst_ref=recv1.at[me], send_sem=s1, recv_sem=r1,
            device_id={"ctx": to}, device_id_type=MESH,
        ).start()
    recv1[pl.ds(me, 1)] = send1[pl.ds(me, 1)]

    anti = (iota((LANES, LANES), 0) + iota((LANES, LANES), 1) == LANES - 1).astype(BF16)
    for i in range(chunks):
        at = slice(i * LANES, (i + 1) * LANES)
        xrev[:, at] = nn(xv[:, at], anti).astype(BF16)
    lane = iota((LANES, LANES), 1)
    sub = iota((LANES, LANES), 0)
    later = lane >= sub
    low = iota((modes, LANES), 1) % per_group < per_group // 2
    for g in range(groups):
        at = slice(g * per_group, (g + 1) * per_group)
        left = jnp.concatenate([gv[at, j * LANES : (j + 1) * LANES] for j in range(chunks)], axis=0)
        right = jnp.concatenate(
            [
                jnp.concatenate(
                    [
                        xrev[at, (j - b) * LANES : (j - b + 1) * LANES] if b <= j else jnp.zeros((per_group, LANES), BF16)
                        for b in range(chunks)
                    ],
                    axis=1,
                )
                for j in range(chunks)
            ],
            axis=0,
        )
        pairs = tn(left, right)
        turned = [
            pltpu.roll(pairs[:, b * LANES : (b + 1) * LANES], 0, axis=1, stride=1, stride_axis=0)
            for b in range(chunks)
        ]
        zero = jnp.zeros((LANES, LANES), F32)
        for b in range(chunks + 1):
            here = turned[b] if b < chunks else zero
            before = turned[b - 1] if b > 0 else zero
            lagv[g : g + 1, b * LANES : (b + 1) * LANES] = jnp.sum(jnp.where(later, here, before), axis=0, keepdims=True)
    zero_lane = iota((groups, LANES), 1) == 0
    lags = [pltpu.roll(lagv[:, b * LANES : (b + 1) * LANES], 1, axis=1) for b in range(chunks + 1)]
    lags = jnp.concatenate([jnp.where(zero_lane, lags[b], lags[b + 1]) for b in range(chunks)], axis=1)
    for g in range(groups):
        at = slice(g * modes, (g + 1) * modes)
        e = fwd[at, :] * lags[g : g + 1, :]
        w = e * lane_pos
        e = sum(e[:, b * LANES : (b + 1) * LANES] for b in range(chunks))
        w = sum(w[:, b * LANES : (b + 1) * LANES] for b in range(chunks))
        for shift in (64, 32, 16, 8):
            e = e + pltpu.roll(e, shift, axis=1)
            w = w + pltpu.roll(w, shift, axis=1)
        both = jnp.where(low, e, w)
        for h in range(modes // 8):
            k = g * (modes // 8) + h
            sendl[k] = jnp.sum(jnp.where(own_segment, both[h * 8 : (h + 1) * 8], 0.0), axis=0, keepdims=True)
    for i in range(1, parts):
        to = wrap(me + i, parts)
        pltpu.make_async_remote_copy(
            src_ref=sendl.at[to], dst_ref=recvl.at[me], send_sem=sl, recv_sem=rl,
            device_id={"ctx": to}, device_id_type=MESH,
        ).start()
    recvl[pl.ds(me, 1)] = sendl[pl.ds(me, 1)]

    mine = dcol[pl.ds(pl.multiple_of(me * 8, 8), 8), :]
    seg = me * 8 // modes % (LANES // per_group)
    dl = jnp.sum(jnp.where(segment == (iota((8, LANES), 0) + seg) % 8, mine, 0.0), axis=0, keepdims=True)
    all_wait(recv1.at[pl.ds(0, parts - 1)], r1)
    gs, gt, xs, xt = (recv1[:, kind, :] for kind in range(4))
    n = 1
    while n < parts:
        factor = jnp.exp(-(dl * float(n * width)))
        ahead = down(gs, n)
        gt = gt + factor * (down(gt, n) + float(n * width) * ahead)
        gs = gs + factor * ahead
        n *= 2
    gs, gt = down(gs, 1), down(gt, 1)
    for p in range(parts):
        send2[p, 0:1, :] = gs[p : p + 1, :]
    plain = jnp.sum(xs * gs, axis=0, keepdims=True)
    weighted = jnp.sum(xs * gt + xt * gs, axis=0, keepdims=True)
    plain = plain + pltpu.roll(plain, LANES - per_group // 2, axis=1)
    weighted = weighted + pltpu.roll(weighted, per_group // 2, axis=1)
    all_wait(recvl.at[pl.ds(0, parts - 1)], rl)
    local = jnp.sum(recvl[...], axis=0)
    first_half = iota((1, LANES), 1) % per_group < per_group // 2
    pair_row = pltpu.roll(jnp.where(first_half, plain, weighted), (8 - seg) % 8 * per_group, axis=1) + local
    for p in range(parts):
        send2[p, 1:2, :] = pair_row
    for i in range(1, parts):
        to = wrap(me + i, parts)
        pltpu.make_async_remote_copy(
            src_ref=send2.at[to], dst_ref=recv2.at[me], send_sem=s2, recv_sem=r2,
            device_id={"ctx": to}, device_id_type=MESH,
        ).start()
    recv2[pl.ds(me, 1)] = send2[pl.ds(me, 1)]

    for g in range(groups):
        at = slice(g * modes, (g + 1) * modes)
        w = jnp.concatenate([rcol[at, :]] * chunks, axis=1) * bwd[at, :]
        wout[at, :], wout[rows + g * modes : rows + (g + 1) * modes, :] = split(w)
        hrow[g : g + 1, :width] = jnp.sum(w, axis=0, keepdims=True)
        start = jnp.sum(rcol[at, :], axis=0, keepdims=True)
        hrow[g : g + 1, width:] = jnp.where(iota((1, LANES), 1) == 0, start, 0.0)
    for g in range(groups):
        at = slice(g * per_group, (g + 1) * per_group)
        turned = [
            pltpu.roll(
                jnp.broadcast_to(hrow[g : g + 1, b * LANES : (b + 1) * LANES], (LANES, LANES)),
                0, axis=1, stride=1, stride_axis=0,
            )
            for b in range(chunks + 1)
        ]
        blocks = [
            jnp.concatenate(split(jnp.where(later, turned[chunks - b], turned[chunks - 1 - b])), axis=1)
            for b in range(chunks)
        ]
        right = jnp.concatenate(blocks, axis=0)
        left = jnp.concatenate(
            [
                gv[at, :] if i == 0 else jnp.concatenate(
                    [gv[at, i * LANES :], jnp.zeros((per_group, i * LANES), BF16)], axis=1
                )
                for i in range(chunks)
            ],
            axis=0,
        )
        o = nn(left, right)
        o = o[:, :LANES] + o[:, LANES:]
        for i in range(chunks):
            outl[at, i * LANES : (i + 1) * LANES] = o[i * per_group : (i + 1) * per_group, :]
    rx[...] = jnp.zeros_like(rx)

    all_wait(recv2.at[pl.ds(0, parts - 1)], r2)
    from_lane, to_lane = iota((LANES, LANES), 0), iota((LANES, LANES), 1)
    same_mode = from_lane // per_group == to_lane % 8
    kind_of = (from_lane % per_group >= per_group // 2) == (to_lane >= LANES // 2)
    select = jnp.where(same_mode & kind_of & (to_lane % (LANES // 2) < modes), 1.0, 0.0)
    sums = jnp.dot(recv2[:, 1, :], select, precision=HIGH, preferred_element_type=F32)
    sums = jnp.where(iota((parts, LANES), 0) % 2 == iota((parts, LANES), 1) % modes // 8, sums, 0.0)
    fold = (iota((groups, parts), 0) == iota((groups, parts), 1) // 2).astype(F32)
    send3[...] = jnp.dot(fold, sums, precision=HIGH, preferred_element_type=F32)
    for i in range(1, batch):
        to = wrap(row_of + i, batch)
        pltpu.make_async_remote_copy(
            src_ref=send3, dst_ref=recv3.at[row_of], send_sem=s3, recv_sem=r3,
            device_id={"dp": to}, device_id_type=MESH,
        ).start()
    recv3[pl.ds(row_of, 1)] = send3[...][None]

    for k in range(parts):
        first = (k * 8 // modes) * per_group
        half, seg = first // LANES, (first % LANES) // per_group
        v = jnp.broadcast_to(recv2[k, 0:1, :], (8, LANES))
        v = jnp.where(turned_segment[seg], v, 0.0)
        for shift in (64, 32, 16):
            v = v + pltpu.roll(v, shift, axis=1)
        v = jnp.where(segment == seg, v, 0.0)
        rx[k * 8 : (k + 1) * 8, half * LANES : (half + 1) * LANES] = v
    r_top, r_low = split(rx[...])
    w_top, w_low = wout[:rows, :], wout[rows:, :]
    far = tn(jnp.concatenate([r_top, r_top, r_low], axis=0), jnp.concatenate([w_top, w_low, w_top], axis=0))
    outv[...] = (outl[...] + far).astype(BF16)
    store = pltpu.make_async_copy(outv, out_hbm.at[0], out_sem.at[0])
    store.start()

    all_wait(recv3.at[pl.ds(0, batch - 1)], r3)
    total = recv3[0]
    for b in range(1, batch):
        total = total + recv3[b]
    pv[...] = total[:, :modes] * (norm * scale)
    qv[...] = total[:, LANES // 2 : LANES // 2 + modes] * (dec * norm * scale)
    more = [pltpu.make_async_copy(pv, p_hbm, out_sem.at[1]), pltpu.make_async_copy(qv, q_hbm, out_sem.at[2])]
    for copy in more:
        copy.start()
    all_wait(send1.at[pl.ds(0, parts - 1)], s1)
    all_wait(sendl.at[pl.ds(0, parts - 1)], sl)
    all_wait(send2.at[pl.ds(0, parts - 1)], s2)
    all_wait(recv3.at[pl.ds(0, batch - 1)], s3)
    store.wait()
    for copy in more:
        copy.wait()


def on_device(parts, batch, signal, grad_out, residue, decay):
    _, chans, width = signal.shape
    groups, modes = residue.shape
    per_group = chans // groups
    rows = groups * modes
    scale = 1.0 / math.sqrt(per_group * batch * parts * width)
    dims = (parts, batch, groups, modes, per_group, width, scale)
    vm = pltpu.VMEM
    return pl.pallas_call(
        functools.partial(kernel, dims),
        out_shape=(
            jax.ShapeDtypeStruct(signal.shape, BF16),
            jax.ShapeDtypeStruct((groups, modes), F32),
            jax.ShapeDtypeStruct((groups, modes), F32),
        ),
        in_specs=[pl.BlockSpec(memory_space=pl.ANY)] * 4,
        out_specs=[pl.BlockSpec(memory_space=pl.ANY)] * 3,
        scratch_shapes=[
            vm((chans, width), BF16), vm((chans, width), BF16), vm((groups, modes), F32), vm((groups, modes), F32),
            vm((rows, LANES), F32), vm((rows, LANES), F32),
            vm((2 * rows, 2 * width), BF16), vm((2 * rows, 2 * width), BF16),
            vm((rows, width), F32), vm((rows, width), F32),
            vm((2 * rows, chans), F32), vm((2 * rows, chans), F32),
            vm((2 * rows, width), BF16), vm((groups, width + LANES), F32),
            vm((chans, width), BF16), vm((groups, width + LANES), F32),
            vm((chans, width), F32), vm((rows, chans), F32), vm((chans, width), BF16),
            vm((groups, modes), F32), vm((groups, modes), F32),
            vm((parts, 4, LANES), F32), vm((parts, 4, LANES), F32),
            vm((parts, 1, LANES), F32), vm((parts, 1, LANES), F32),
            vm((parts, 2, LANES), F32), vm((parts, 2, LANES), F32),
            vm((groups, LANES), F32), vm((batch, groups, LANES), F32),
            pltpu.SemaphoreType.DMA((4,)), pltpu.SemaphoreType.DMA((3,)),
        ] + [pltpu.SemaphoreType.DMA] * 8,
        compiler_params=pltpu.CompilerParams(
            collective_id=0, has_side_effects=True, vmem_limit_bytes=40 * 1024 * 1024
        ),
    )(signal, grad_out, residue, decay)


def solution(mesh):
    placed = (P("dp", None, "ctx"), P("dp", None, "ctx"), P(), P())
    return jax.shard_map(
        functools.partial(on_device, mesh.shape["ctx"], mesh.shape["dp"]),
        mesh=mesh,
        in_specs=placed,
        out_specs=(P("dp", None, "ctx"), P(), P()),
        check_vma=False,
    )
```

```python
import functools
import math

import jax
import jax.numpy as jnp
from jax import lax
from jax.experimental import pallas as pl
from jax.experimental.pallas import tpu as pltpu
from jax.sharding import PartitionSpec as P

MESH = pl.DeviceIdType.MESH
F32 = jnp.float32
BF16 = jnp.bfloat16
LANES = 128
OWNERS = 4
HIGH = lax.Precision.HIGHEST


def iota(shape, dim):
    return lax.broadcasted_iota(jnp.int32, shape, dim)


def split(value):
    top = value.astype(BF16)
    return top, (value - top.astype(F32)).astype(BF16)


def wrap(value, size):
    return jnp.where(value >= size, value - size, value)


def down(value, rows):
    return jnp.concatenate([value[rows:], jnp.zeros((rows, value.shape[1]), value.dtype)], axis=0)


def nt(left, right):
    return lax.dot_general(left, right, (((1,), (1,)), ((), ())), preferred_element_type=F32)


def tn(left, right):
    return lax.dot_general(left, right, (((0,), (0,)), ((), ())), preferred_element_type=F32)


def nn(left, right):
    return jnp.dot(left, right, preferred_element_type=F32)


def all_wait(ref, sem):
    pltpu.make_async_copy(ref, ref, sem).wait()


def greet(barrier, axis, me, size):
    for i in range(1, size):
        pl.semaphore_signal(barrier, inc=1, device_id={axis: wrap(me + i, size)}, device_id_type=MESH)


def send(src, dst, send_sem, recv_sem, axis, to):
    pltpu.make_async_remote_copy(
        src_ref=src, dst_ref=dst, send_sem=send_sem, recv_sem=recv_sem, device_id={axis: to}, device_id_type=MESH
    ).start()


def scatter(src_of, dst, send_sem, recv_sem, axis, me, size):
    for i in range(1, size):
        to = wrap(me + i, size)
        send(src_of(to), dst, send_sem, recv_sem, axis, to)


def kernel(
    dims, x_hbm, g_hbm, res_hbm, dec_hbm, outv, pv, qv,
    xv, gv, resv, decv, dcol, rcol, lg, lx, fwd, bwd, yg, yx, wout, hrow, xrev, lagv, outl, rx,
    send1, recv1, sendl, recvl, send2, recv2, send3, recv3, send4, recv4,
    in_sem, s1, r1, sl, rl, s2, r2, s3, r3, s4, r4,
):
    parts, batch, groups, modes, per_group, width, scale = dims
    rows = groups * modes
    chunks = width // LANES
    me = lax.axis_index("ctx")
    row_of = lax.axis_index("dp")
    owners, share = recv2.shape[0], recv2.shape[1]
    run = owners // 2
    owner_ids = [o // run * (parts // 2) + o % run for o in range(owners)]
    slot = me // (parts // 2) * run + me % (parts // 2)
    is_owner = me % (parts // 2) < run
    plain = jnp.logical_not(is_owner)

    def gather(src, dst, send_sem, recv_sem):
        for o, to in enumerate(owner_ids):
            pl.when(me != to)(functools.partial(send, src.at[o], dst.at[me], send_sem, recv_sem, "ctx", to))


    loads = []
    for i, (src, dst) in enumerate(
        ((dec_hbm, decv), (res_hbm, resv), (g_hbm.at[0], gv), (x_hbm.at[0], xv))
    ):
        loads.append(pltpu.make_async_copy(src, dst, in_sem.at[i]))
        loads[-1].start()
    barrier = pltpu.get_barrier_semaphore()

    @pl.when(is_owner)
    def _():
        greet(barrier, "ctx", me, parts)
        greet(barrier, "dp", row_of, batch)

    loads[0].wait()
    loads[1].wait()
    dec = decv[...]
    series = dec * dec
    series = 1.0 + series / 6.0 * (1.0 + series / 20.0 * (1.0 + series / 42.0 * (1.0 + series / 72.0)))
    norm = jnp.sqrt(2.0 * jnp.exp(-dec) * dec * series)
    eye = iota((modes, modes), 0) == iota((modes, modes), 1)
    for g in range(groups):
        at = slice(g * modes, (g + 1) * modes)
        for src, dst in ((dec, dcol), (resv[...] * norm, rcol)):
            column = jnp.sum(jnp.where(eye, src[g : g + 1, :], 0.0), axis=1, keepdims=True)
            dst[at, :] = jnp.broadcast_to(column, (modes, LANES))

    lane_pos = iota((modes, width), 1).astype(F32)
    back_pos = width - lane_pos
    for g in range(groups):
        at = slice(g * modes, (g + 1) * modes)
        second = slice(rows + g * modes, rows + (g + 1) * modes)
        d = jnp.concatenate([dcol[at, :]] * chunks, axis=1)
        for pos, keep, dst in ((lane_pos, fwd, lg), (back_pos, bwd, lx)):
            e = jnp.exp(-(d * pos))
            keep[at, :] = e
            dst[at, :width], dst[at, width:] = split(e)
            dst[second, :width], dst[second, width:] = split(e * pos)

    loads[2].wait()
    yg[...] = nt(lg[...], jnp.concatenate([gv[...], gv[...]], axis=1))
    loads[3].wait()
    yx[...] = nt(lx[...], jnp.concatenate([xv[...], xv[...]], axis=1))

    segment = iota((8, LANES), 1) // per_group
    own_segment = segment == iota((8, LANES), 0)
    turned_segment = [segment == (iota((8, LANES), 0) + seg) % 8 for seg in range(8)]
    for k in range(parts):
        first = (k * 8 // modes) * per_group
        half, seg = first // LANES, (first % LANES) // per_group
        for kind, src in enumerate((yg, yg, yx, yx)):
            r0 = (kind % 2) * rows + k * 8
            v = src[r0 : r0 + 8, half * LANES : (half + 1) * LANES]
            v = pltpu.roll(v, 0, axis=1, stride=per_group, stride_axis=0)
            send1[k // share, k % share, kind : kind + 1, :] = jnp.sum(jnp.where(turned_segment[seg], v, 0.0), axis=0, keepdims=True)

    pl.when(is_owner)(lambda: pl.semaphore_wait(barrier, owners - 1 + batch - 1))
    pl.when(plain)(lambda: pl.semaphore_wait(barrier, owners))
    gather(send1, recv1, s1, r1)

    anti = (iota((LANES, LANES), 0) + iota((LANES, LANES), 1) == LANES - 1).astype(BF16)
    for i in range(chunks):
        at = slice(i * LANES, (i + 1) * LANES)
        xrev[:, at] = nn(xv[:, at], anti).astype(BF16)
    lane = iota((LANES, LANES), 1)
    sub = iota((LANES, LANES), 0)
    later = lane >= sub
    low = iota((modes, LANES), 1) % per_group < per_group // 2
    for g in range(groups):
        at = slice(g * per_group, (g + 1) * per_group)
        left = jnp.concatenate([gv[at, j * LANES : (j + 1) * LANES] for j in range(chunks)], axis=0)
        right = jnp.concatenate(
            [
                jnp.concatenate(
                    [
                        xrev[at, (j - b) * LANES : (j - b + 1) * LANES] if b <= j else jnp.zeros((per_group, LANES), BF16)
                        for b in range(chunks)
                    ],
                    axis=1,
                )
                for j in range(chunks)
            ],
            axis=0,
        )
        pairs = tn(left, right)
        turned = [
            pltpu.roll(pairs[:, b * LANES : (b + 1) * LANES], 0, axis=1, stride=1, stride_axis=0)
            for b in range(chunks)
        ]
        zero = jnp.zeros((LANES, LANES), F32)
        for b in range(chunks + 1):
            here = turned[b] if b < chunks else zero
            before = turned[b - 1] if b > 0 else zero
            lagv[g : g + 1, b * LANES : (b + 1) * LANES] = jnp.sum(jnp.where(later, here, before), axis=0, keepdims=True)
    zero_lane = iota((groups, LANES), 1) == 0
    lags = [pltpu.roll(lagv[:, b * LANES : (b + 1) * LANES], 1, axis=1) for b in range(chunks + 1)]
    lags = jnp.concatenate([jnp.where(zero_lane, lags[b], lags[b + 1]) for b in range(chunks)], axis=1)
    for g in range(groups):
        at = slice(g * modes, (g + 1) * modes)
        e = fwd[at, :] * lags[g : g + 1, :]
        w = e * lane_pos
        e = sum(e[:, b * LANES : (b + 1) * LANES] for b in range(chunks))
        w = sum(w[:, b * LANES : (b + 1) * LANES] for b in range(chunks))
        for shift in (64, 32, 16, 8):
            e = e + pltpu.roll(e, shift, axis=1)
            w = w + pltpu.roll(w, shift, axis=1)
        both = jnp.where(low, e, w)
        for h in range(modes // 8):
            k = g * (modes // 8) + h
            sendl[k // share, k % share : k % share + 1, :] = jnp.sum(jnp.where(own_segment, both[h * 8 : (h + 1) * 8], 0.0), axis=0, keepdims=True)
    gather(sendl, recvl, sl, rl)

    for g in range(groups):
        at = slice(g * modes, (g + 1) * modes)
        w = jnp.concatenate([rcol[at, :]] * chunks, axis=1) * bwd[at, :]
        wout[at, :], wout[rows + g * modes : rows + (g + 1) * modes, :] = split(w)
        hrow[g : g + 1, :width] = jnp.sum(w, axis=0, keepdims=True)
        start = jnp.sum(rcol[at, :], axis=0, keepdims=True)
        hrow[g : g + 1, width:] = jnp.where(iota((1, LANES), 1) == 0, start, 0.0)
    for g in range(groups):
        at = slice(g * per_group, (g + 1) * per_group)
        turned = [
            pltpu.roll(
                jnp.broadcast_to(hrow[g : g + 1, b * LANES : (b + 1) * LANES], (LANES, LANES)),
                0, axis=1, stride=1, stride_axis=0,
            )
            for b in range(chunks + 1)
        ]
        blocks = [
            jnp.concatenate(split(jnp.where(later, turned[chunks - b], turned[chunks - 1 - b])), axis=1)
            for b in range(chunks)
        ]
        right = jnp.concatenate(blocks, axis=0)
        left = jnp.concatenate(
            [
                gv[at, :] if i == 0 else jnp.concatenate(
                    [gv[at, i * LANES :], jnp.zeros((per_group, i * LANES), BF16)], axis=1
                )
                for i in range(chunks)
            ],
            axis=0,
        )
        o = nn(left, right)
        o = o[:, :LANES] + o[:, LANES:]
        for i in range(chunks):
            outl[at, i * LANES : (i + 1) * LANES] = o[i * per_group : (i + 1) * per_group, :]
    rx[...] = jnp.zeros_like(rx)

    @pl.when(is_owner)
    def _():
        recv1[pl.ds(me, 1)] = send1[pl.ds(slot, 1)]
        recvl[pl.ds(me, 1)] = sendl[pl.ds(slot, 1)]
        all_wait(recv1.at[pl.ds(0, parts - 1)], r1)
        first_half = iota((1, LANES), 1) % per_group < per_group // 2
        for j in range(share):
            k = slot * share + j
            seg = k * 8 // modes % (LANES // per_group)
            mine = dcol[pl.ds(pl.multiple_of(k * 8, 8), 8), :]
            dl = jnp.sum(jnp.where(segment == (iota((8, LANES), 0) + seg) % 8, mine, 0.0), axis=0, keepdims=True)
            gs, gt, xs, xt = (recv1[:, j, kind, :] for kind in range(4))
            n = 1
            while n < parts:
                factor = jnp.exp(-(dl * float(n * width)))
                ahead = down(gs, n)
                gt = gt + factor * (down(gt, n) + float(n * width) * ahead)
                gs = gs + factor * ahead
                n *= 2
            gs, gt = down(gs, 1), down(gt, 1)
            send2[:, j, :] = gs
            one = jnp.sum(xs * gs, axis=0, keepdims=True)
            two = jnp.sum(xs * gt + xt * gs, axis=0, keepdims=True)
            one = one + pltpu.roll(one, LANES - per_group // 2, axis=1)
            two = two + pltpu.roll(two, per_group // 2, axis=1)
            send3[j : j + 1, :] = pltpu.roll(jnp.where(first_half, one, two), (8 - seg) % 8 * per_group, axis=1)
        recv2[pl.ds(slot, 1)] = send2[pl.ds(me, 1)]
        all_wait(recvl.at[pl.ds(0, parts - 1)], rl)
        send3[...] = send3[...] + jnp.sum(recvl[...], axis=0)
        recv3[pl.ds(row_of, 1)] = send3[...][None]
        scatter(lambda to: send3, recv3.at[row_of], s3, r3, "dp", row_of, batch)
        scatter(lambda to: send2.at[to], recv2.at[slot], s2, r2, "ctx", me, parts)
        all_wait(recv3.at[pl.ds(0, batch - 1)], r3)
        total = recv3[0]
        for b in range(1, batch):
            total = total + recv3[b]
        send4[...] = total
        recv4[pl.ds(slot, 1)] = total[None]
        scatter(lambda to: send4, recv4.at[slot], s4, r4, "ctx", me, parts)
        all_wait(recv2.at[pl.ds(0, owners - 1)], r2)

    pl.when(plain)(lambda: all_wait(recv2, r2))

    for k in range(parts):
        first = (k * 8 // modes) * per_group
        half, seg = first // LANES, (first % LANES) // per_group
        v = jnp.broadcast_to(recv2[k // share, k % share : k % share + 1, :], (8, LANES))
        v = jnp.where(turned_segment[seg], v, 0.0)
        for shift in (64, 32, 16):
            v = v + pltpu.roll(v, shift, axis=1)
        v = jnp.where(segment == seg, v, 0.0)
        rx[k * 8 : (k + 1) * 8, half * LANES : (half + 1) * LANES] = v
    r_top, r_low = split(rx[...])
    w_top, w_low = wout[:rows, :], wout[rows:, :]
    far = tn(jnp.concatenate([r_top, r_top, r_low], axis=0), jnp.concatenate([w_top, w_low, w_top], axis=0))
    outv[0] = (outl[...] + far).astype(BF16)

    from_lane, to_lane = iota((LANES, LANES), 0), iota((LANES, LANES), 1)
    same_mode = from_lane // per_group == to_lane % 8
    kind_of = (from_lane % per_group >= per_group // 2) == (to_lane >= LANES // 2)
    select = jnp.where(same_mode & kind_of & (to_lane % (LANES // 2) < modes), 1.0, 0.0)
    fold = (iota((groups, parts), 0) == iota((groups, parts), 1) // 2).astype(F32)
    pl.when(is_owner)(lambda: all_wait(recv4.at[pl.ds(0, owners - 1)], r4))
    pl.when(plain)(lambda: all_wait(recv4, r4))
    sums = jnp.concatenate([recv4[o] for o in range(owners)], axis=0)
    sums = jnp.dot(sums, select, precision=HIGH, preferred_element_type=F32)
    sums = jnp.where(iota((parts, LANES), 0) % 2 == iota((parts, LANES), 1) % modes // 8, sums, 0.0)
    total = jnp.dot(fold, sums, precision=HIGH, preferred_element_type=F32)
    pv[...] = total[:, :modes] * (norm * scale)
    qv[...] = total[:, LANES // 2 : LANES // 2 + modes] * (dec * norm * scale)

    @pl.when(is_owner)
    def _():
        all_wait(send1.at[pl.ds(0, owners - 1)], s1)
        all_wait(sendl.at[pl.ds(0, owners - 1)], sl)
        all_wait(send2.at[pl.ds(0, parts - 1)], s2)
        all_wait(recv3.at[pl.ds(0, batch - 1)], s3)
        all_wait(recvl.at[pl.ds(0, parts - 1)], s4)

    @pl.when(plain)
    def _():
        all_wait(send1, s1)
        all_wait(sendl, sl)


def on_device(parts, batch, signal, grad_out, residue, decay):
    _, chans, width = signal.shape
    groups, modes = residue.shape
    per_group = chans // groups
    rows = groups * modes
    scale = 1.0 / math.sqrt(per_group * batch * parts * width)
    owners = OWNERS
    share = rows // 8 // owners
    dims = (parts, batch, groups, modes, per_group, width, scale)
    vm = pltpu.VMEM
    shapes = (
        jax.ShapeDtypeStruct(signal.shape, BF16),
        jax.ShapeDtypeStruct((groups, modes), F32),
        jax.ShapeDtypeStruct((groups, modes), F32),
    )
    return pl.pallas_call(
        functools.partial(kernel, dims),
        out_shape=tuple(vm(shape.shape, shape.dtype) for shape in shapes),
        in_specs=[pl.BlockSpec(memory_space=pl.ANY)] * 4,
        out_specs=[pl.BlockSpec(memory_space=vm)] * 3,
        scratch_shapes=[
            vm((chans, width), BF16), vm((chans, width), BF16), vm((groups, modes), F32), vm((groups, modes), F32),
            vm((rows, LANES), F32), vm((rows, LANES), F32),
            vm((2 * rows, 2 * width), BF16), vm((2 * rows, 2 * width), BF16),
            vm((rows, width), F32), vm((rows, width), F32),
            vm((2 * rows, chans), F32), vm((2 * rows, chans), F32),
            vm((2 * rows, width), BF16), vm((groups, width + LANES), F32),
            vm((chans, width), BF16), vm((groups, width + LANES), F32),
            vm((chans, width), F32), vm((rows, chans), F32),
            vm((owners, share, 4, LANES), F32), vm((parts, share, 4, LANES), F32),
            vm((owners, share, LANES), F32), vm((parts, share, LANES), F32),
            vm((parts, share, LANES), F32), vm((owners, share, LANES), F32),
            vm((share, LANES), F32), vm((batch, share, LANES), F32),
            vm((share, LANES), F32), vm((owners, share, LANES), F32),
            pltpu.SemaphoreType.DMA((4,)),
        ] + [pltpu.SemaphoreType.DMA] * 10,
        compiler_params=pltpu.CompilerParams(
            collective_id=0, has_side_effects=True, vmem_limit_bytes=60 * 1024 * 1024
        ),
    )(signal, grad_out, residue, decay)


def solution(mesh):
    placed = (P("dp", None, "ctx"), P("dp", None, "ctx"), P(), P())
    return jax.shard_map(
        functools.partial(on_device, mesh.shape["ctx"], mesh.shape["dp"]),
        mesh=mesh,
        in_specs=placed,
        out_specs=(P("dp", None, "ctx"), P(), P()),
        check_vma=False,
    )
```

```python
import functools
import math

import jax
import jax.numpy as jnp
from jax import lax
from jax.experimental import pallas as pl
from jax.experimental.pallas import tpu as pltpu
from jax.sharding import PartitionSpec as P

MESH = pl.DeviceIdType.MESH
F32 = jnp.float32
BF16 = jnp.bfloat16
LANES = 128
OWNERS = 4
HIGH = lax.Precision.HIGHEST


def iota(shape, dim):
    return lax.broadcasted_iota(jnp.int32, shape, dim)


def split(value):
    top = value.astype(BF16)
    return top, (value - top.astype(F32)).astype(BF16)


def wrap(value, size):
    return jnp.where(value >= size, value - size, value)


def down(value, rows):
    return jnp.concatenate([value[rows:], jnp.zeros((rows, value.shape[1]), value.dtype)], axis=0)


def nt(left, right):
    return lax.dot_general(left, right, (((1,), (1,)), ((), ())), preferred_element_type=F32)


def tn(left, right):
    return lax.dot_general(left, right, (((0,), (0,)), ((), ())), preferred_element_type=F32)


def nn(left, right):
    return jnp.dot(left, right, preferred_element_type=F32)


def all_wait(ref, sem):
    pltpu.make_async_copy(ref, ref, sem).wait()


def greet(barrier, axis, me, size):
    for i in range(1, size):
        pl.semaphore_signal(barrier, inc=1, device_id={axis: wrap(me + i, size)}, device_id_type=MESH)


def send(src, dst, send_sem, recv_sem, axis, to):
    pltpu.make_async_remote_copy(
        src_ref=src, dst_ref=dst, send_sem=send_sem, recv_sem=recv_sem, device_id={axis: to}, device_id_type=MESH
    ).start()


def scatter(src_of, dst, send_sem, recv_sem, axis, me, size):
    for i in range(1, size):
        to = wrap(me + i, size)
        send(src_of(to), dst, send_sem, recv_sem, axis, to)


def kernel(
    dims, x_hbm, g_hbm, res_hbm, dec_hbm, outv, pv, qv,
    xv, gv, resv, decv, dcol, rcol, lg, lx, fwd, bwd, yg, yx, wout, hrow, xrev, lagv, outl, rx,
    send1, recv1, sendl, recvl, send2, recv2, send3, recv3, send4, recv4,
    in_sem, s1, r1, sl, rl, s2, r2, s3, r3, s4, r4,
):
    parts, batch, groups, modes, per_group, width, scale = dims
    rows = groups * modes
    chunks = width // LANES
    me = lax.axis_index("ctx")
    row_of = lax.axis_index("dp")
    owners, share = recv2.shape[0], recv2.shape[1]
    run = owners // 2
    owner_ids = [o // run * (parts // 2) + o % run for o in range(owners)]
    slot = me // (parts // 2) * run + me % (parts // 2)
    is_owner = me % (parts // 2) < run
    plain = jnp.logical_not(is_owner)

    def gather(src, dst, send_sem, recv_sem):
        for o, to in enumerate(owner_ids):
            pl.when(me != to)(functools.partial(send, src.at[o], dst.at[me], send_sem, recv_sem, "ctx", to))


    loads = []
    for i, (src, dst) in enumerate(
        ((dec_hbm, decv), (res_hbm, resv), (g_hbm.at[0], gv), (x_hbm.at[0], xv))
    ):
        loads.append(pltpu.make_async_copy(src, dst, in_sem.at[i]))
        loads[-1].start()
    barrier = pltpu.get_barrier_semaphore()

    @pl.when(is_owner)
    def _():
        greet(barrier, "ctx", me, parts)
        greet(barrier, "dp", row_of, batch)

    loads[0].wait()
    loads[1].wait()
    dec = decv[...]
    series = dec * dec
    series = 1.0 + series / 6.0 * (1.0 + series / 20.0 * (1.0 + series / 42.0 * (1.0 + series / 72.0)))
    norm = jnp.sqrt(2.0 * jnp.exp(-dec) * dec * series)
    eye = iota((modes, modes), 0) == iota((modes, modes), 1)
    for g in range(groups):
        at = slice(g * modes, (g + 1) * modes)
        for src, dst in ((dec, dcol), (resv[...] * norm, rcol)):
            column = jnp.sum(jnp.where(eye, src[g : g + 1, :], 0.0), axis=1, keepdims=True)
            dst[at, :] = jnp.broadcast_to(column, (modes, LANES))

    lane_pos = iota((modes, width), 1).astype(F32)
    back_pos = width - lane_pos
    for g in range(groups):
        at = slice(g * modes, (g + 1) * modes)
        second = slice(rows + g * modes, rows + (g + 1) * modes)
        d = jnp.concatenate([dcol[at, :]] * chunks, axis=1)
        for pos, keep, dst in ((lane_pos, fwd, lg), (back_pos, bwd, lx)):
            e = jnp.exp(-(d * pos))
            keep[at, :] = e
            dst[at, :width], dst[at, width:] = split(e)
            dst[second, :width], dst[second, width:] = split(e * pos)

    loads[2].wait()
    yg[...] = nt(lg[...], jnp.concatenate([gv[...], gv[...]], axis=1))
    loads[3].wait()
    yx[...] = nt(lx[...], jnp.concatenate([xv[...], xv[...]], axis=1))

    segment = iota((8, LANES), 1) // per_group
    own_segment = segment == iota((8, LANES), 0)
    turned_segment = [segment == (iota((8, LANES), 0) + seg) % 8 for seg in range(8)]
    for k in range(parts):
        first = (k * 8 // modes) * per_group
        half, seg = first // LANES, (first % LANES) // per_group
        for kind, src in enumerate((yg, yg, yx, yx)):
            r0 = (kind % 2) * rows + k * 8
            v = src[r0 : r0 + 8, half * LANES : (half + 1) * LANES]
            v = pltpu.roll(v, 0, axis=1, stride=per_group, stride_axis=0)
            send1[k // share, k % share, kind : kind + 1, :] = jnp.sum(jnp.where(turned_segment[seg], v, 0.0), axis=0, keepdims=True)

    pl.when(is_owner)(lambda: pl.semaphore_wait(barrier, owners - 1 + batch - 1))
    pl.when(plain)(lambda: pl.semaphore_wait(barrier, owners))
    gather(send1, recv1, s1, r1)

    anti = (iota((LANES, LANES), 0) + iota((LANES, LANES), 1) == LANES - 1).astype(BF16)
    for i in range(chunks):
        at = slice(i * LANES, (i + 1) * LANES)
        xrev[:, at] = nn(xv[:, at], anti).astype(BF16)
    lane = iota((LANES, LANES), 1)
    sub = iota((LANES, LANES), 0)
    later = lane >= sub
    low = iota((modes, LANES), 1) % per_group < per_group // 2
    for g in range(groups):
        at = slice(g * per_group, (g + 1) * per_group)
        left = jnp.concatenate([gv[at, j * LANES : (j + 1) * LANES] for j in range(chunks)], axis=0)
        right = jnp.concatenate(
            [
                jnp.concatenate(
                    [
                        xrev[at, (j - b) * LANES : (j - b + 1) * LANES] if b <= j else jnp.zeros((per_group, LANES), BF16)
                        for b in range(chunks)
                    ],
                    axis=1,
                )
                for j in range(chunks)
            ],
            axis=0,
        )
        pairs = tn(left, right)
        turned = [
            pltpu.roll(pairs[:, b * LANES : (b + 1) * LANES], 0, axis=1, stride=1, stride_axis=0)
            for b in range(chunks)
        ]
        zero = jnp.zeros((LANES, LANES), F32)
        for b in range(chunks + 1):
            here = turned[b] if b < chunks else zero
            before = turned[b - 1] if b > 0 else zero
            lagv[g : g + 1, b * LANES : (b + 1) * LANES] = jnp.sum(jnp.where(later, here, before), axis=0, keepdims=True)
    zero_lane = iota((groups, LANES), 1) == 0
    lags = [pltpu.roll(lagv[:, b * LANES : (b + 1) * LANES], 1, axis=1) for b in range(chunks + 1)]
    lags = jnp.concatenate([jnp.where(zero_lane, lags[b], lags[b + 1]) for b in range(chunks)], axis=1)
    for g in range(groups):
        at = slice(g * modes, (g + 1) * modes)
        e = fwd[at, :] * lags[g : g + 1, :]
        w = e * lane_pos
        e = sum(e[:, b * LANES : (b + 1) * LANES] for b in range(chunks))
        w = sum(w[:, b * LANES : (b + 1) * LANES] for b in range(chunks))
        for shift in (64, 32, 16, 8):
            e = e + pltpu.roll(e, shift, axis=1)
            w = w + pltpu.roll(w, shift, axis=1)
        both = jnp.where(low, e, w)
        for h in range(modes // 8):
            k = g * (modes // 8) + h
            sendl[k // share, k % share : k % share + 1, :] = jnp.sum(jnp.where(own_segment, both[h * 8 : (h + 1) * 8], 0.0), axis=0, keepdims=True)
    gather(sendl, recvl, sl, rl)

    for g in range(groups):
        at = slice(g * modes, (g + 1) * modes)
        w = jnp.concatenate([rcol[at, :]] * chunks, axis=1) * bwd[at, :]
        wout[at, :], wout[rows + g * modes : rows + (g + 1) * modes, :] = split(w)
        hrow[g : g + 1, :width] = jnp.sum(w, axis=0, keepdims=True)
        start = jnp.sum(rcol[at, :], axis=0, keepdims=True)
        hrow[g : g + 1, width:] = jnp.where(iota((1, LANES), 1) == 0, start, 0.0)
    for g in range(groups):
        at = slice(g * per_group, (g + 1) * per_group)
        turned = [
            pltpu.roll(
                jnp.broadcast_to(hrow[g : g + 1, b * LANES : (b + 1) * LANES], (LANES, LANES)),
                0, axis=1, stride=1, stride_axis=0,
            )
            for b in range(chunks + 1)
        ]
        blocks = [
            jnp.concatenate(split(jnp.where(later, turned[chunks - b], turned[chunks - 1 - b])), axis=1)
            for b in range(chunks)
        ]
        right = jnp.concatenate(blocks, axis=0)
        left = jnp.concatenate(
            [
                gv[at, :] if i == 0 else jnp.concatenate(
                    [gv[at, i * LANES :], jnp.zeros((per_group, i * LANES), BF16)], axis=1
                )
                for i in range(chunks)
            ],
            axis=0,
        )
        o = nn(left, right)
        o = o[:, :LANES] + o[:, LANES:]
        for i in range(chunks):
            outl[at, i * LANES : (i + 1) * LANES] = o[i * per_group : (i + 1) * per_group, :]
    rx[...] = jnp.zeros_like(rx)

    @pl.when(is_owner)
    def _():
        recv1[pl.ds(me, 1)] = send1[pl.ds(slot, 1)]
        recvl[pl.ds(me, 1)] = sendl[pl.ds(slot, 1)]
        all_wait(recv1.at[pl.ds(0, parts - 1)], r1)
        first_half = iota((1, LANES), 1) % per_group < per_group // 2
        for j in range(share):
            k = slot * share + j
            seg = k * 8 // modes % (LANES // per_group)
            mine = dcol[pl.ds(pl.multiple_of(k * 8, 8), 8), :]
            dl = jnp.sum(jnp.where(segment == (iota((8, LANES), 0) + seg) % 8, mine, 0.0), axis=0, keepdims=True)
            gs, gt, xs, xt = (recv1[:, j, kind, :] for kind in range(4))
            n = 1
            while n < parts:
                factor = jnp.exp(-(dl * float(n * width)))
                ahead = down(gs, n)
                gt = gt + factor * (down(gt, n) + float(n * width) * ahead)
                gs = gs + factor * ahead
                n *= 2
            gs, gt = down(gs, 1), down(gt, 1)
            send2[:, j, :] = gs
            one = jnp.sum(xs * gs, axis=0, keepdims=True)
            two = jnp.sum(xs * gt + xt * gs, axis=0, keepdims=True)
            one = one + pltpu.roll(one, LANES - per_group // 2, axis=1)
            two = two + pltpu.roll(two, per_group // 2, axis=1)
            send3[j : j + 1, :] = pltpu.roll(jnp.where(first_half, one, two), (8 - seg) % 8 * per_group, axis=1)
        recv2[pl.ds(slot, 1)] = send2[pl.ds(me, 1)]
        all_wait(recvl.at[pl.ds(0, parts - 1)], rl)
        send3[...] = send3[...] + jnp.sum(recvl[...], axis=0)
        recv3[pl.ds(row_of, 1)] = send3[...][None]
        scatter(lambda to: send3, recv3.at[row_of], s3, r3, "dp", row_of, batch)
        scatter(lambda to: send2.at[to], recv2.at[slot], s2, r2, "ctx", me, parts)
        all_wait(recv3.at[pl.ds(0, batch - 1)], r3)
        total = recv3[0]
        for b in range(1, batch):
            total = total + recv3[b]
        send4[...] = total
        recv4[pl.ds(slot, 1)] = total[None]
        scatter(lambda to: send4, recv4.at[slot], s4, r4, "ctx", me, parts)
        all_wait(recv2.at[pl.ds(0, owners - 1)], r2)

    pl.when(plain)(lambda: all_wait(recv2, r2))

    for k in range(parts):
        first = (k * 8 // modes) * per_group
        half, seg = first // LANES, (first % LANES) // per_group
        v = jnp.broadcast_to(recv2[k // share, k % share : k % share + 1, :], (8, LANES))
        v = jnp.where(turned_segment[seg], v, 0.0)
        for shift in (64, 32, 16):
            v = v + pltpu.roll(v, shift, axis=1)
        v = jnp.where(segment == seg, v, 0.0)
        rx[k * 8 : (k + 1) * 8, half * LANES : (half + 1) * LANES] = v
    r_top, r_low = split(rx[...])
    w_top, w_low = wout[:rows, :], wout[rows:, :]
    far = tn(jnp.concatenate([r_top, r_top, r_low], axis=0), jnp.concatenate([w_top, w_low, w_top], axis=0))
    outv[0] = (outl[...] + far).astype(BF16)

    from_lane, to_lane = iota((LANES, LANES), 0), iota((LANES, LANES), 1)
    same_mode = from_lane // per_group == to_lane % 8
    kind_of = (from_lane % per_group >= per_group // 2) == (to_lane >= LANES // 2)
    select = jnp.where(same_mode & kind_of & (to_lane % (LANES // 2) < modes), 1.0, 0.0)
    fold = (iota((groups, parts), 0) == iota((groups, parts), 1) // 2).astype(F32)
    pl.when(is_owner)(lambda: all_wait(recv4.at[pl.ds(0, owners - 1)], r4))
    pl.when(plain)(lambda: all_wait(recv4, r4))
    sums = jnp.concatenate([recv4[o] for o in range(owners)], axis=0)
    sums = jnp.dot(sums, select, precision=HIGH, preferred_element_type=F32)
    sums = jnp.where(iota((parts, LANES), 0) % 2 == iota((parts, LANES), 1) % modes // 8, sums, 0.0)
    total = jnp.dot(fold, sums, precision=HIGH, preferred_element_type=F32)
    pv[...] = total[:, :modes] * (norm * scale)
    qv[...] = total[:, LANES // 2 : LANES // 2 + modes] * (dec * norm * scale)

    @pl.when(is_owner)
    def _():
        all_wait(send1.at[pl.ds(0, owners - 1)], s1)
        all_wait(sendl.at[pl.ds(0, owners - 1)], sl)
        all_wait(send2.at[pl.ds(0, parts - 1)], s2)
        all_wait(recv3.at[pl.ds(0, batch - 1)], s3)
        all_wait(recvl.at[pl.ds(0, parts - 1)], s4)

    @pl.when(plain)
    def _():
        all_wait(send1, s1)
        all_wait(sendl, sl)


def finish(*refs):
    copies = [pltpu.make_async_copy(refs[i], refs[3 + i], refs[6].at[i]) for i in range(3)]
    for copy in copies:
        copy.start()
    for copy in copies:
        copy.wait()


def on_device(parts, batch, signal, grad_out, residue, decay):
    _, chans, width = signal.shape
    groups, modes = residue.shape
    per_group = chans // groups
    rows = groups * modes
    scale = 1.0 / math.sqrt(per_group * batch * parts * width)
    owners = OWNERS
    share = rows // 8 // owners
    dims = (parts, batch, groups, modes, per_group, width, scale)
    vm = pltpu.VMEM
    shapes = (
        jax.ShapeDtypeStruct(signal.shape, BF16),
        jax.ShapeDtypeStruct((groups, modes), F32),
        jax.ShapeDtypeStruct((groups, modes), F32),
    )
    results = pl.pallas_call(
        functools.partial(kernel, dims),
        out_shape=tuple(vm(shape.shape, shape.dtype) for shape in shapes),
        in_specs=[pl.BlockSpec(memory_space=pl.ANY)] * 4,
        out_specs=[pl.BlockSpec(memory_space=vm)] * 3,
        scratch_shapes=[
            vm((chans, width), BF16), vm((chans, width), BF16), vm((groups, modes), F32), vm((groups, modes), F32),
            vm((rows, LANES), F32), vm((rows, LANES), F32),
            vm((2 * rows, 2 * width), BF16), vm((2 * rows, 2 * width), BF16),
            vm((rows, width), F32), vm((rows, width), F32),
            vm((2 * rows, chans), F32), vm((2 * rows, chans), F32),
            vm((2 * rows, width), BF16), vm((groups, width + LANES), F32),
            vm((chans, width), BF16), vm((groups, width + LANES), F32),
            vm((chans, width), F32), vm((rows, chans), F32),
            vm((owners, share, 4, LANES), F32), vm((parts, share, 4, LANES), F32),
            vm((owners, share, LANES), F32), vm((parts, share, LANES), F32),
            vm((parts, share, LANES), F32), vm((owners, share, LANES), F32),
            vm((share, LANES), F32), vm((batch, share, LANES), F32),
            vm((share, LANES), F32), vm((owners, share, LANES), F32),
            pltpu.SemaphoreType.DMA((4,)),
        ] + [pltpu.SemaphoreType.DMA] * 10,
        compiler_params=pltpu.CompilerParams(
            collective_id=0, has_side_effects=True, vmem_limit_bytes=60 * 1024 * 1024
        ),
    )(signal, grad_out, residue, decay)
    return pl.pallas_call(
        finish,
        out_shape=shapes,
        in_specs=[pl.BlockSpec(memory_space=vm)] * 3,
        out_specs=[pl.BlockSpec(memory_space=pl.ANY)] * 3,
        scratch_shapes=[pltpu.SemaphoreType.DMA((3,))],
        compiler_params=pltpu.CompilerParams(vmem_limit_bytes=4 * 1024 * 1024),
    )(*results)


def solution(mesh):
    placed = (P("dp", None, "ctx"), P("dp", None, "ctx"), P(), P())
    return jax.shard_map(
        functools.partial(on_device, mesh.shape["ctx"], mesh.shape["dp"]),
        mesh=mesh,
        in_specs=placed,
        out_specs=(P("dp", None, "ctx"), P(), P()),
        check_vma=False,
    )
```

```python
import functools
import math

import jax
import jax.numpy as jnp
from jax import lax
from jax.experimental import pallas as pl
from jax.experimental.pallas import tpu as pltpu
from jax.sharding import PartitionSpec as P

MESH = pl.DeviceIdType.MESH
F32 = jnp.float32
BF16 = jnp.bfloat16
LANES = 128
OWNERS = 8
HIGH = lax.Precision.HIGHEST


def iota(shape, dim):
    return lax.broadcasted_iota(jnp.int32, shape, dim)


def split(value):
    top = value.astype(BF16)
    return top, (value - top.astype(F32)).astype(BF16)


def wrap(value, size):
    return jnp.where(value >= size, value - size, value)


def down(value, rows):
    return jnp.concatenate([value[rows:], jnp.zeros((rows, value.shape[1]), value.dtype)], axis=0)


def nt(left, right):
    return lax.dot_general(left, right, (((1,), (1,)), ((), ())), preferred_element_type=F32)


def tn(left, right):
    return lax.dot_general(left, right, (((0,), (0,)), ((), ())), preferred_element_type=F32)


def nn(left, right):
    return jnp.dot(left, right, preferred_element_type=F32)


def all_wait(ref, sem):
    pltpu.make_async_copy(ref, ref, sem).wait()


def greet(barrier, axis, me, size):
    for i in range(1, size):
        pl.semaphore_signal(barrier, inc=1, device_id={axis: wrap(me + i, size)}, device_id_type=MESH)


def send(src, dst, send_sem, recv_sem, axis, to):
    pltpu.make_async_remote_copy(
        src_ref=src, dst_ref=dst, send_sem=send_sem, recv_sem=recv_sem, device_id={axis: to}, device_id_type=MESH
    ).start()


def scatter(src_of, dst, send_sem, recv_sem, axis, me, size):
    for i in range(1, size):
        to = wrap(me + i, size)
        send(src_of(to), dst, send_sem, recv_sem, axis, to)


def kernel(
    dims, x_hbm, g_hbm, res_hbm, dec_hbm, outv, pv, qv,
    xv, gv, resv, decv, dcol, rcol, lg, lx, fwd, bwd, yg, yx, wout, hrow, xrev, lagv, outl, rx,
    send1, recv1, sendl, recvl, send2, recv2, send3, recv3, send4, recv4,
    in_sem, s1, r1, sl, rl, s2, r2, s3, r3, s4, r4,
):
    parts, batch, groups, modes, per_group, width, scale = dims
    rows = groups * modes
    chunks = width // LANES
    me = lax.axis_index("ctx")
    row_of = lax.axis_index("dp")
    owners, share = recv2.shape[0], recv2.shape[1]
    run = owners // 2
    owner_ids = [o // run * (parts // 2) + o % run for o in range(owners)]
    slot = me // (parts // 2) * run + me % (parts // 2)
    is_owner = me % (parts // 2) < run
    plain = jnp.logical_not(is_owner)

    def gather(src, dst, send_sem, recv_sem):
        for o, to in enumerate(owner_ids):
            pl.when(me != to)(functools.partial(send, src.at[o], dst.at[me], send_sem, recv_sem, "ctx", to))


    loads = []
    for i, (src, dst) in enumerate(
        ((dec_hbm, decv), (res_hbm, resv), (g_hbm.at[0], gv), (x_hbm.at[0], xv))
    ):
        loads.append(pltpu.make_async_copy(src, dst, in_sem.at[i]))
        loads[-1].start()
    barrier = pltpu.get_barrier_semaphore()

    @pl.when(is_owner)
    def _():
        greet(barrier, "ctx", me, parts)
        greet(barrier, "dp", row_of, batch)

    eye = iota((modes, modes), 0) == iota((modes, modes), 1)

    def columns(src, dst):
        for g in range(groups):
            column = jnp.sum(jnp.where(eye, src[g : g + 1, :], 0.0), axis=1, keepdims=True)
            dst[g * modes : (g + 1) * modes, :] = jnp.broadcast_to(column, (modes, LANES))

    loads[0].wait()
    dec = decv[...]
    columns(dec, dcol)

    lane_pos = iota((modes, width), 1).astype(F32)
    back_pos = width - lane_pos
    for g in range(groups):
        at = slice(g * modes, (g + 1) * modes)
        second = slice(rows + g * modes, rows + (g + 1) * modes)
        d = jnp.concatenate([dcol[at, :]] * chunks, axis=1)
        for pos, keep, dst in ((lane_pos, fwd, lg), (back_pos, bwd, lx)):
            e = jnp.exp(-(d * pos))
            keep[at, :] = e
            dst[at, :width], dst[at, width:] = split(e)
            dst[second, :width], dst[second, width:] = split(e * pos)

    loads[2].wait()
    yg[...] = nt(lg[...], jnp.concatenate([gv[...], gv[...]], axis=1))
    loads[3].wait()
    yx[...] = nt(lx[...], jnp.concatenate([xv[...], xv[...]], axis=1))

    segment = iota((8, LANES), 1) // per_group
    own_segment = segment == iota((8, LANES), 0)
    turned_segment = [segment == (iota((8, LANES), 0) + seg) % 8 for seg in range(8)]
    for k in range(parts):
        first = (k * 8 // modes) * per_group
        half, seg = first // LANES, (first % LANES) // per_group
        for kind, src in enumerate((yg, yg, yx, yx)):
            r0 = (kind % 2) * rows + k * 8
            v = src[r0 : r0 + 8, half * LANES : (half + 1) * LANES]
            v = pltpu.roll(v, 0, axis=1, stride=per_group, stride_axis=0)
            send1[k // share, k % share, kind : kind + 1, :] = jnp.sum(jnp.where(turned_segment[seg], v, 0.0), axis=0, keepdims=True)

    pl.when(is_owner)(lambda: pl.semaphore_wait(barrier, owners - 1 + batch - 1))
    pl.when(plain)(lambda: pl.semaphore_wait(barrier, owners))
    gather(send1, recv1, s1, r1)

    anti = (iota((LANES, LANES), 0) + iota((LANES, LANES), 1) == LANES - 1).astype(BF16)
    for i in range(chunks):
        at = slice(i * LANES, (i + 1) * LANES)
        xrev[:, at] = nn(xv[:, at], anti).astype(BF16)
    lane = iota((LANES, LANES), 1)
    sub = iota((LANES, LANES), 0)
    wanted = (lane < sub) | (lane == LANES - 1)
    low = iota((modes, LANES), 1) % per_group < per_group // 2
    lane_chunk = iota((modes, LANES), 1) // per_group
    near = iota((modes, LANES), 1).astype(F32)

    def stack(ref, at):
        return jnp.concatenate([ref[at, j * LANES : (j + 1) * LANES] for j in range(chunks)], axis=0)

    def both(ref, at, start):
        return jnp.concatenate(
            [ref[at, start : start + LANES], ref[at, width + start : width + start + LANES]], axis=1
        )

    for g in range(groups):
        at = slice(g * per_group, (g + 1) * per_group)
        turned = pltpu.roll(tn(stack(gv, at), stack(xrev, at)), 0, axis=1, stride=1, stride_axis=0)
        lagv[g : g + 1, :] = jnp.sum(jnp.where(wanted, turned, 0.0), axis=0, keepdims=True)
    for g in range(groups):
        at = slice(g * modes, (g + 1) * modes)
        second = slice(rows + g * modes, rows + (g + 1) * modes)
        chans = slice(g * per_group, (g + 1) * per_group)
        weights = jnp.concatenate(
            [both(lg, at, 0), both(lg, second, 0), both(lx, at, width - LANES), both(lx, second, width - LANES)],
            axis=0,
        )
        data = jnp.concatenate([stack(gv, chans), stack(xv, chans)], axis=0)
        o = nt(weights, jnp.concatenate([data, data], axis=1))
        gs, gt = o[:modes], o[modes : 2 * modes]
        xs, xt = (pltpu.roll(o[j * modes : (j + 1) * modes], LANES // 2, axis=1) for j in (2, 3))
        lam = jnp.exp(-(dcol[at, :] * float(LANES)))
        factor, r, rt = 1.0, 0.0, 0.0
        for n in range(1, chunks):
            known = lane_chunk < chunks - n
            a = jnp.where(known, pltpu.roll(gs, LANES - n * per_group, axis=1), 0.0)
            at_n = jnp.where(known, pltpu.roll(gt, LANES - n * per_group, axis=1), 0.0)
            r = r + factor * a
            rt = rt + factor * (at_n + float((n - 1) * LANES) * a)
            factor = factor * lam
        e = fwd[at, :LANES] * pltpu.roll(lagv[g : g + 1, :], 1, axis=1)
        w = e * near + (xs * rt + xt * r)
        e = e + xs * r
        for shift in (64, 32, 16, 8):
            e = e + pltpu.roll(e, shift, axis=1)
            w = w + pltpu.roll(w, shift, axis=1)
        mixed = jnp.where(low, e, w)
        for h in range(modes // 8):
            k = g * (modes // 8) + h
            sendl[k // share, k % share : k % share + 1, :] = jnp.sum(
                jnp.where(own_segment, mixed[h * 8 : (h + 1) * 8], 0.0), axis=0, keepdims=True
            )
    gather(sendl, recvl, sl, rl)

    loads[1].wait()
    series = dec * dec
    series = 1.0 + series / 6.0 * (1.0 + series / 20.0 * (1.0 + series / 42.0 * (1.0 + series / 72.0)))
    norm = jnp.sqrt(2.0 * jnp.exp(-dec) * dec * series)
    columns(resv[...] * norm, rcol)
    later = lane >= sub

    for g in range(groups):
        at = slice(g * modes, (g + 1) * modes)
        w = jnp.concatenate([rcol[at, :]] * chunks, axis=1) * bwd[at, :]
        wout[at, :], wout[rows + g * modes : rows + (g + 1) * modes, :] = split(w)
        hrow[g : g + 1, :width] = jnp.sum(w, axis=0, keepdims=True)
        start = jnp.sum(rcol[at, :], axis=0, keepdims=True)
        hrow[g : g + 1, width:] = jnp.where(iota((1, LANES), 1) == 0, start, 0.0)
    for g in range(groups):
        at = slice(g * per_group, (g + 1) * per_group)
        turned = [
            pltpu.roll(
                jnp.broadcast_to(hrow[g : g + 1, b * LANES : (b + 1) * LANES], (LANES, LANES)),
                0, axis=1, stride=1, stride_axis=0,
            )
            for b in range(chunks + 1)
        ]
        blocks = [
            jnp.concatenate(split(jnp.where(later, turned[chunks - b], turned[chunks - 1 - b])), axis=1)
            for b in range(chunks)
        ]
        right = jnp.concatenate(blocks, axis=0)
        left = jnp.concatenate(
            [
                gv[at, :] if i == 0 else jnp.concatenate(
                    [gv[at, i * LANES :], jnp.zeros((per_group, i * LANES), BF16)], axis=1
                )
                for i in range(chunks)
            ],
            axis=0,
        )
        o = nn(left, right)
        o = o[:, :LANES] + o[:, LANES:]
        for i in range(chunks):
            outl[at, i * LANES : (i + 1) * LANES] = o[i * per_group : (i + 1) * per_group, :]
    rx[...] = jnp.zeros_like(rx)

    @pl.when(is_owner)
    def _():
        recv1[pl.ds(me, 1)] = send1[pl.ds(slot, 1)]
        recvl[pl.ds(me, 1)] = sendl[pl.ds(slot, 1)]
        all_wait(recv1.at[pl.ds(0, parts - 1)], r1)
        first_half = iota((1, LANES), 1) % per_group < per_group // 2
        for j in range(share):
            k = slot * share + j
            seg = k * 8 // modes % (LANES // per_group)
            mine = dcol[pl.ds(pl.multiple_of(k * 8, 8), 8), :]
            dl = jnp.sum(jnp.where(segment == (iota((8, LANES), 0) + seg) % 8, mine, 0.0), axis=0, keepdims=True)
            gs, gt, xs, xt = (recv1[:, j, kind, :] for kind in range(4))
            n = 1
            while n < parts:
                factor = jnp.exp(-(dl * float(n * width)))
                ahead = down(gs, n)
                gt = gt + factor * (down(gt, n) + float(n * width) * ahead)
                gs = gs + factor * ahead
                n *= 2
            gs, gt = down(gs, 1), down(gt, 1)
            send2[:, j, :] = gs
            one = jnp.sum(xs * gs, axis=0, keepdims=True)
            two = jnp.sum(xs * gt + xt * gs, axis=0, keepdims=True)
            one = one + pltpu.roll(one, LANES - per_group // 2, axis=1)
            two = two + pltpu.roll(two, per_group // 2, axis=1)
            send3[j : j + 1, :] = pltpu.roll(jnp.where(first_half, one, two), (8 - seg) % 8 * per_group, axis=1)
        recv2[pl.ds(slot, 1)] = send2[pl.ds(me, 1)]
        all_wait(recvl.at[pl.ds(0, parts - 1)], rl)
        send3[...] = send3[...] + jnp.sum(recvl[...], axis=0)
        recv3[pl.ds(row_of, 1)] = send3[...][None]
        scatter(lambda to: send3, recv3.at[row_of], s3, r3, "dp", row_of, batch)
        scatter(lambda to: send2.at[to], recv2.at[slot], s2, r2, "ctx", me, parts)
        all_wait(recv3.at[pl.ds(0, batch - 1)], r3)
        total = recv3[0]
        for b in range(1, batch):
            total = total + recv3[b]
        send4[...] = total
        recv4[pl.ds(slot, 1)] = total[None]
        scatter(lambda to: send4, recv4.at[slot], s4, r4, "ctx", me, parts)
        all_wait(recv2.at[pl.ds(0, owners - 1)], r2)

    pl.when(plain)(lambda: all_wait(recv2, r2))

    for k in range(parts):
        first = (k * 8 // modes) * per_group
        half, seg = first // LANES, (first % LANES) // per_group
        v = jnp.broadcast_to(recv2[k // share, k % share : k % share + 1, :], (8, LANES))
        v = jnp.where(turned_segment[seg], v, 0.0)
        for shift in (64, 32, 16):
            v = v + pltpu.roll(v, shift, axis=1)
        v = jnp.where(segment == seg, v, 0.0)
        rx[k * 8 : (k + 1) * 8, half * LANES : (half + 1) * LANES] = v
    r_top, r_low = split(rx[...])
    w_top, w_low = wout[:rows, :], wout[rows:, :]
    far = tn(jnp.concatenate([r_top, r_top, r_low], axis=0), jnp.concatenate([w_top, w_low, w_top], axis=0))
    outv[0] = (outl[...] + far).astype(BF16)

    from_lane, to_lane = iota((LANES, LANES), 0), iota((LANES, LANES), 1)
    same_mode = from_lane // per_group == to_lane % 8
    kind_of = (from_lane % per_group >= per_group // 2) == (to_lane >= LANES // 2)
    select = jnp.where(same_mode & kind_of & (to_lane % (LANES // 2) < modes), 1.0, 0.0)
    fold = (iota((groups, parts), 0) == iota((groups, parts), 1) // 2).astype(F32)
    pl.when(is_owner)(lambda: all_wait(recv4.at[pl.ds(0, owners - 1)], r4))
    pl.when(plain)(lambda: all_wait(recv4, r4))
    sums = jnp.concatenate([recv4[o] for o in range(owners)], axis=0)
    sums = jnp.dot(sums, select, precision=HIGH, preferred_element_type=F32)
    sums = jnp.where(iota((parts, LANES), 0) % 2 == iota((parts, LANES), 1) % modes // 8, sums, 0.0)
    total = jnp.dot(fold, sums, precision=HIGH, preferred_element_type=F32)
    pv[...] = total[:, :modes] * (norm * scale)
    qv[...] = total[:, LANES // 2 : LANES // 2 + modes] * (dec * norm * scale)

    @pl.when(is_owner)
    def _():
        all_wait(send1.at[pl.ds(0, owners - 1)], s1)
        all_wait(sendl.at[pl.ds(0, owners - 1)], sl)
        all_wait(send2.at[pl.ds(0, parts - 1)], s2)
        all_wait(recv3.at[pl.ds(0, batch - 1)], s3)
        all_wait(recvl.at[pl.ds(0, parts - 1)], s4)

    @pl.when(plain)
    def _():
        all_wait(send1, s1)
        all_wait(sendl, sl)


def finish(*refs):
    copies = [pltpu.make_async_copy(refs[i], refs[3 + i], refs[6].at[i]) for i in range(3)]
    for copy in copies:
        copy.start()
    for copy in copies:
        copy.wait()


def on_device(parts, batch, signal, grad_out, residue, decay):
    _, chans, width = signal.shape
    groups, modes = residue.shape
    per_group = chans // groups
    rows = groups * modes
    scale = 1.0 / math.sqrt(per_group * batch * parts * width)
    owners = OWNERS
    share = rows // 8 // owners
    dims = (parts, batch, groups, modes, per_group, width, scale)
    vm = pltpu.VMEM
    shapes = (
        jax.ShapeDtypeStruct(signal.shape, BF16),
        jax.ShapeDtypeStruct((groups, modes), F32),
        jax.ShapeDtypeStruct((groups, modes), F32),
    )
    results = pl.pallas_call(
        functools.partial(kernel, dims),
        out_shape=tuple(vm(shape.shape, shape.dtype) for shape in shapes),
        in_specs=[pl.BlockSpec(memory_space=pl.ANY)] * 4,
        out_specs=[pl.BlockSpec(memory_space=vm)] * 3,
        scratch_shapes=[
            vm((chans, width), BF16), vm((chans, width), BF16), vm((groups, modes), F32), vm((groups, modes), F32),
            vm((rows, LANES), F32), vm((rows, LANES), F32),
            vm((2 * rows, 2 * width), BF16), vm((2 * rows, 2 * width), BF16),
            vm((rows, width), F32), vm((rows, width), F32),
            vm((2 * rows, chans), F32), vm((2 * rows, chans), F32),
            vm((2 * rows, width), BF16), vm((groups, width + LANES), F32),
            vm((chans, width), BF16), vm((groups, LANES), F32),
            vm((chans, width), F32), vm((rows, chans), F32),
            vm((owners, share, 4, LANES), F32), vm((parts, share, 4, LANES), F32),
            vm((owners, share, LANES), F32), vm((parts, share, LANES), F32),
            vm((parts, share, LANES), F32), vm((owners, share, LANES), F32),
            vm((share, LANES), F32), vm((batch, share, LANES), F32),
            vm((share, LANES), F32), vm((owners, share, LANES), F32),
            pltpu.SemaphoreType.DMA((4,)),
        ] + [pltpu.SemaphoreType.DMA] * 10,
        compiler_params=pltpu.CompilerParams(
            collective_id=0, has_side_effects=True, vmem_limit_bytes=60 * 1024 * 1024
        ),
    )(signal, grad_out, residue, decay)
    return pl.pallas_call(
        finish,
        out_shape=shapes,
        in_specs=[pl.BlockSpec(memory_space=vm)] * 3,
        out_specs=[pl.BlockSpec(memory_space=pl.ANY)] * 3,
        scratch_shapes=[pltpu.SemaphoreType.DMA((3,))],
        compiler_params=pltpu.CompilerParams(vmem_limit_bytes=4 * 1024 * 1024),
    )(*results)


def solution(mesh):
    placed = (P("dp", None, "ctx"), P("dp", None, "ctx"), P(), P())
    return jax.shard_map(
        functools.partial(on_device, mesh.shape["ctx"], mesh.shape["dp"]),
        mesh=mesh,
        in_specs=placed,
        out_specs=(P("dp", None, "ctx"), P(), P()),
        check_vma=False,
    )
```

```python
import functools
import math

import jax
import jax.numpy as jnp
from jax import lax
from jax.experimental import pallas as pl
from jax.experimental.pallas import tpu as pltpu
from jax.sharding import PartitionSpec as P

MESH = pl.DeviceIdType.MESH
F32 = jnp.float32
BF16 = jnp.bfloat16
LANES = 128
OWNERS = 8
HIGH = lax.Precision.HIGHEST


def iota(shape, dim):
    return lax.broadcasted_iota(jnp.int32, shape, dim)


def split(value):
    top = value.astype(BF16)
    return top, (value - top.astype(F32)).astype(BF16)


def wrap(value, size):
    return jnp.where(value >= size, value - size, value)


def down(value, rows):
    return jnp.concatenate([value[rows:], jnp.zeros((rows, value.shape[1]), value.dtype)], axis=0)


def nt(left, right):
    return lax.dot_general(left, right, (((1,), (1,)), ((), ())), preferred_element_type=F32)


def tn(left, right):
    return lax.dot_general(left, right, (((0,), (0,)), ((), ())), preferred_element_type=F32)


def nn(left, right):
    return jnp.dot(left, right, preferred_element_type=F32)


def all_wait(ref, sem):
    pltpu.make_async_copy(ref, ref, sem).wait()


def greet(barrier, axis, me, size):
    for i in range(1, size):
        pl.semaphore_signal(barrier, inc=1, device_id={axis: wrap(me + i, size)}, device_id_type=MESH)


def send(src, dst, send_sem, recv_sem, axis, to):
    pltpu.make_async_remote_copy(
        src_ref=src, dst_ref=dst, send_sem=send_sem, recv_sem=recv_sem, device_id={axis: to}, device_id_type=MESH
    ).start()


def scatter(src_of, dst, send_sem, recv_sem, axis, me, size):
    for i in range(1, size):
        to = wrap(me + i, size)
        send(src_of(to), dst, send_sem, recv_sem, axis, to)


def kernel(
    dims, x_hbm, g_hbm, res_hbm, dec_hbm, outv, pv, qv,
    xv, gv, resv, decv, dcol, rcol, wts, fwd, parts_of, wout, hrow, xrev, lagv, outl, rx,
    send1, recv1, sendl, recvl, send2, recv2, send3, recv3, send4, recv4,
    in_sem, s1, r1, sl, rl, s2, r2, s3, r3, s4, r4,
):
    parts, batch, groups, modes, per_group, width, scale = dims
    rows = groups * modes
    chunks = width // LANES
    me = lax.axis_index("ctx")
    row_of = lax.axis_index("dp")
    owners, share = recv2.shape[0], recv2.shape[1]
    run = owners // 2
    owner_ids = [o // run * (parts // 2) + o % run for o in range(owners)]
    slot = me // (parts // 2) * run + me % (parts // 2)
    is_owner = me % (parts // 2) < run
    plain = jnp.logical_not(is_owner)

    def gather(src, dst, send_sem, recv_sem):
        for o, to in enumerate(owner_ids):
            pl.when(me != to)(functools.partial(send, src.at[o], dst.at[me], send_sem, recv_sem, "ctx", to))


    loads = []
    for i, (src, dst) in enumerate(
        ((dec_hbm, decv), (res_hbm, resv), (g_hbm.at[0], gv), (x_hbm.at[0], xv))
    ):
        loads.append(pltpu.make_async_copy(src, dst, in_sem.at[i]))
        loads[-1].start()
    barrier = pltpu.get_barrier_semaphore()

    @pl.when(is_owner)
    def _():
        greet(barrier, "ctx", me, parts)
        greet(barrier, "dp", row_of, batch)

    eye = iota((modes, modes), 0) == iota((modes, modes), 1)

    def columns(src, dst):
        for g in range(groups):
            column = jnp.sum(jnp.where(eye, src[g : g + 1, :], 0.0), axis=1, keepdims=True)
            dst[g * modes : (g + 1) * modes, :] = jnp.broadcast_to(column, (modes, LANES))

    loads[0].wait()
    dec = decv[...]
    columns(dec, dcol)

    lane = iota((modes, LANES), 1)
    near = lane.astype(F32)
    away = LANES - near
    for g in range(groups):
        at = slice(g * modes, (g + 1) * modes)
        e = jnp.exp(-(dcol[at, :] * near))
        f = jnp.exp(-(dcol[at, :] * away))
        fwd[at, :] = e
        for kind, value in enumerate((e, e * near, f, f * away)):
            r0 = (4 * g + kind) * modes
            wts[r0 : r0 + modes, :LANES], wts[r0 : r0 + modes, LANES:] = split(value)

    loads[2].wait()
    loads[3].wait()

    def stack(ref, at):
        return jnp.concatenate([ref[at, j * LANES : (j + 1) * LANES] for j in range(chunks)], axis=0)

    segment = iota((8, LANES), 1) // per_group
    own_segment = segment == iota((8, LANES), 0)
    turned_segment = [segment == (iota((8, LANES), 0) + seg) % 8 for seg in range(8)]
    is_grad = lane < chunks * per_group
    steps = jnp.where(is_grad, lane // per_group, 2 * chunks - 1 - lane // per_group).astype(F32) * float(LANES)
    for g in range(groups):
        at = slice(g * modes, (g + 1) * modes)
        chans = slice(g * per_group, (g + 1) * per_group)
        data = jnp.concatenate([stack(gv, chans), stack(xv, chans)], axis=0)
        o = nt(wts[4 * g * modes : 4 * (g + 1) * modes, :], jnp.concatenate([data, data], axis=1))
        parts_of[4 * g * modes : 4 * (g + 1) * modes, :] = o
        factor = jnp.exp(-(dcol[at, :] * steps))
        gs, gt, xs, xt = (o[kind * modes : (kind + 1) * modes] for kind in range(4))
        for kind, (mask, v) in enumerate(
            ((is_grad, gs), (is_grad, gt + steps * gs), (~is_grad, xs), (~is_grad, xt + steps * xs))
        ):
            v = jnp.where(mask, v * factor, 0.0)
            for shift in (64, 32, 16):
                v = v + pltpu.roll(v, shift, axis=1)
            for h in range(modes // 8):
                k = g * (modes // 8) + h
                seg = g % (LANES // per_group)
                send1[k // share, k % share, kind : kind + 1, :] = jnp.sum(
                    jnp.where(turned_segment[seg], v[h * 8 : (h + 1) * 8], 0.0), axis=0, keepdims=True
                )

    pl.when(is_owner)(lambda: pl.semaphore_wait(barrier, owners - 1 + batch - 1))
    pl.when(plain)(lambda: pl.semaphore_wait(barrier, owners))
    gather(send1, recv1, s1, r1)

    anti = (iota((LANES, LANES), 0) + iota((LANES, LANES), 1) == LANES - 1).astype(BF16)
    for i in range(chunks):
        at = slice(i * LANES, (i + 1) * LANES)
        xrev[:, at] = nn(xv[:, at], anti).astype(BF16)
    square_lane = iota((LANES, LANES), 1)
    sub = iota((LANES, LANES), 0)
    wanted = (square_lane < sub) | (square_lane == LANES - 1)
    low = lane % per_group < per_group // 2
    lane_chunk = lane // per_group

    for g in range(groups):
        at = slice(g * per_group, (g + 1) * per_group)
        turned = pltpu.roll(tn(stack(gv, at), stack(xrev, at)), 0, axis=1, stride=1, stride_axis=0)
        lagv[g : g + 1, :] = jnp.sum(jnp.where(wanted, turned, 0.0), axis=0, keepdims=True)
    for g in range(groups):
        at = slice(g * modes, (g + 1) * modes)
        o = parts_of[4 * g * modes : 4 * (g + 1) * modes, :]
        gs, gt = o[:modes], o[modes : 2 * modes]
        xs, xt = (pltpu.roll(o[j * modes : (j + 1) * modes], LANES // 2, axis=1) for j in (2, 3))
        lam = jnp.exp(-(dcol[at, :] * float(LANES)))
        factor, r, rt = 1.0, 0.0, 0.0
        for n in range(1, chunks):
            known = lane_chunk < chunks - n
            a = jnp.where(known, pltpu.roll(gs, LANES - n * per_group, axis=1), 0.0)
            at_n = jnp.where(known, pltpu.roll(gt, LANES - n * per_group, axis=1), 0.0)
            r = r + factor * a
            rt = rt + factor * (at_n + float((n - 1) * LANES) * a)
            factor = factor * lam
        e = fwd[at, :] * pltpu.roll(lagv[g : g + 1, :], 1, axis=1)
        w = e * near + (xs * rt + xt * r)
        e = e + xs * r
        for shift in (64, 32, 16, 8):
            e = e + pltpu.roll(e, shift, axis=1)
            w = w + pltpu.roll(w, shift, axis=1)
        mixed = jnp.where(low, e, w)
        for h in range(modes // 8):
            k = g * (modes // 8) + h
            sendl[k // share, k % share : k % share + 1, :] = jnp.sum(
                jnp.where(own_segment, mixed[h * 8 : (h + 1) * 8], 0.0), axis=0, keepdims=True
            )
    gather(sendl, recvl, sl, rl)

    loads[1].wait()
    series = dec * dec
    series = 1.0 + series / 6.0 * (1.0 + series / 20.0 * (1.0 + series / 42.0 * (1.0 + series / 72.0)))
    norm = jnp.sqrt(2.0 * jnp.exp(-dec) * dec * series)
    columns(resv[...] * norm, rcol)
    later = square_lane >= sub
    back_pos = width - iota((modes, width), 1).astype(F32)

    for g in range(groups):
        at = slice(g * modes, (g + 1) * modes)
        w = jnp.exp(-(jnp.concatenate([dcol[at, :]] * chunks, axis=1) * back_pos))
        w = jnp.concatenate([rcol[at, :]] * chunks, axis=1) * w
        wout[at, :], wout[rows + g * modes : rows + (g + 1) * modes, :] = split(w)
        hrow[g : g + 1, :width] = jnp.sum(w, axis=0, keepdims=True)
        start = jnp.sum(rcol[at, :], axis=0, keepdims=True)
        hrow[g : g + 1, width:] = jnp.where(iota((1, LANES), 1) == 0, start, 0.0)
    for g in range(groups):
        at = slice(g * per_group, (g + 1) * per_group)
        turned = [
            pltpu.roll(
                jnp.broadcast_to(hrow[g : g + 1, b * LANES : (b + 1) * LANES], (LANES, LANES)),
                0, axis=1, stride=1, stride_axis=0,
            )
            for b in range(chunks + 1)
        ]
        blocks = [
            jnp.concatenate(split(jnp.where(later, turned[chunks - b], turned[chunks - 1 - b])), axis=1)
            for b in range(chunks)
        ]
        right = jnp.concatenate(blocks, axis=0)
        left = jnp.concatenate(
            [
                gv[at, :] if i == 0 else jnp.concatenate(
                    [gv[at, i * LANES :], jnp.zeros((per_group, i * LANES), BF16)], axis=1
                )
                for i in range(chunks)
            ],
            axis=0,
        )
        o = nn(left, right)
        o = o[:, :LANES] + o[:, LANES:]
        for i in range(chunks):
            outl[at, i * LANES : (i + 1) * LANES] = o[i * per_group : (i + 1) * per_group, :]
    rx[...] = jnp.zeros_like(rx)

    @pl.when(is_owner)
    def _():
        recv1[pl.ds(me, 1)] = send1[pl.ds(slot, 1)]
        recvl[pl.ds(me, 1)] = sendl[pl.ds(slot, 1)]
        all_wait(recv1.at[pl.ds(0, parts - 1)], r1)
        first_half = iota((1, LANES), 1) % per_group < per_group // 2
        for j in range(share):
            k = slot * share + j
            seg = k * 8 // modes % (LANES // per_group)
            mine = dcol[pl.ds(pl.multiple_of(k * 8, 8), 8), :]
            dl = jnp.sum(jnp.where(segment == (iota((8, LANES), 0) + seg) % 8, mine, 0.0), axis=0, keepdims=True)
            gs, gt, xs, xt = (recv1[:, j, kind, :] for kind in range(4))
            n = 1
            while n < parts:
                factor = jnp.exp(-(dl * float(n * width)))
                ahead = down(gs, n)
                gt = gt + factor * (down(gt, n) + float(n * width) * ahead)
                gs = gs + factor * ahead
                n *= 2
            gs, gt = down(gs, 1), down(gt, 1)
            send2[:, j, :] = gs
            one = jnp.sum(xs * gs, axis=0, keepdims=True)
            two = jnp.sum(xs * gt + xt * gs, axis=0, keepdims=True)
            one = one + pltpu.roll(one, LANES - per_group // 2, axis=1)
            two = two + pltpu.roll(two, per_group // 2, axis=1)
            send3[j : j + 1, :] = pltpu.roll(jnp.where(first_half, one, two), (8 - seg) % 8 * per_group, axis=1)
        recv2[pl.ds(slot, 1)] = send2[pl.ds(me, 1)]
        all_wait(recvl.at[pl.ds(0, parts - 1)], rl)
        send3[...] = send3[...] + jnp.sum(recvl[...], axis=0)
        recv3[pl.ds(row_of, 1)] = send3[...][None]
        scatter(lambda to: send3, recv3.at[row_of], s3, r3, "dp", row_of, batch)
        scatter(lambda to: send2.at[to], recv2.at[slot], s2, r2, "ctx", me, parts)
        all_wait(recv3.at[pl.ds(0, batch - 1)], r3)
        total = recv3[0]
        for b in range(1, batch):
            total = total + recv3[b]
        send4[...] = total
        recv4[pl.ds(slot, 1)] = total[None]
        scatter(lambda to: send4, recv4.at[slot], s4, r4, "ctx", me, parts)
        all_wait(recv2.at[pl.ds(0, owners - 1)], r2)

    pl.when(plain)(lambda: all_wait(recv2, r2))

    for k in range(parts):
        first = (k * 8 // modes) * per_group
        half, seg = first // LANES, (first % LANES) // per_group
        v = jnp.broadcast_to(recv2[k // share, k % share : k % share + 1, :], (8, LANES))
        v = jnp.where(turned_segment[seg], v, 0.0)
        for shift in (64, 32, 16):
            v = v + pltpu.roll(v, shift, axis=1)
        v = jnp.where(segment == seg, v, 0.0)
        rx[k * 8 : (k + 1) * 8, half * LANES : (half + 1) * LANES] = v
    r_top, r_low = split(rx[...])
    w_top, w_low = wout[:rows, :], wout[rows:, :]
    far = tn(jnp.concatenate([r_top, r_top, r_low], axis=0), jnp.concatenate([w_top, w_low, w_top], axis=0))
    outv[0] = (outl[...] + far).astype(BF16)

    from_lane, to_lane = iota((LANES, LANES), 0), iota((LANES, LANES), 1)
    same_mode = from_lane // per_group == to_lane % 8
    kind_of = (from_lane % per_group >= per_group // 2) == (to_lane >= LANES // 2)
    select = jnp.where(same_mode & kind_of & (to_lane % (LANES // 2) < modes), 1.0, 0.0)
    fold = (iota((groups, parts), 0) == iota((groups, parts), 1) // 2).astype(F32)
    pl.when(is_owner)(lambda: all_wait(recv4.at[pl.ds(0, owners - 1)], r4))
    pl.when(plain)(lambda: all_wait(recv4, r4))
    sums = jnp.concatenate([recv4[o] for o in range(owners)], axis=0)
    sums = jnp.dot(sums, select, precision=HIGH, preferred_element_type=F32)
    sums = jnp.where(iota((parts, LANES), 0) % 2 == iota((parts, LANES), 1) % modes // 8, sums, 0.0)
    total = jnp.dot(fold, sums, precision=HIGH, preferred_element_type=F32)
    pv[...] = total[:, :modes] * (norm * scale)
    qv[...] = total[:, LANES // 2 : LANES // 2 + modes] * (dec * norm * scale)

    @pl.when(is_owner)
    def _():
        all_wait(send1.at[pl.ds(0, owners - 1)], s1)
        all_wait(sendl.at[pl.ds(0, owners - 1)], sl)
        all_wait(send2.at[pl.ds(0, parts - 1)], s2)
        all_wait(recv3.at[pl.ds(0, batch - 1)], s3)
        all_wait(recvl.at[pl.ds(0, parts - 1)], s4)

    @pl.when(plain)
    def _():
        all_wait(send1, s1)
        all_wait(sendl, sl)


def finish(*refs):
    copies = [pltpu.make_async_copy(refs[i], refs[3 + i], refs[6].at[i]) for i in range(3)]
    for copy in copies:
        copy.start()
    for copy in copies:
        copy.wait()


def on_device(parts, batch, signal, grad_out, residue, decay):
    _, chans, width = signal.shape
    groups, modes = residue.shape
    per_group = chans // groups
    rows = groups * modes
    scale = 1.0 / math.sqrt(per_group * batch * parts * width)
    owners = OWNERS
    share = rows // 8 // owners
    dims = (parts, batch, groups, modes, per_group, width, scale)
    vm = pltpu.VMEM
    shapes = (
        jax.ShapeDtypeStruct(signal.shape, BF16),
        jax.ShapeDtypeStruct((groups, modes), F32),
        jax.ShapeDtypeStruct((groups, modes), F32),
    )
    results = pl.pallas_call(
        functools.partial(kernel, dims),
        out_shape=tuple(vm(shape.shape, shape.dtype) for shape in shapes),
        in_specs=[pl.BlockSpec(memory_space=pl.ANY)] * 4,
        out_specs=[pl.BlockSpec(memory_space=vm)] * 3,
        scratch_shapes=[
            vm((chans, width), BF16), vm((chans, width), BF16), vm((groups, modes), F32), vm((groups, modes), F32),
            vm((rows, LANES), F32), vm((rows, LANES), F32),
            vm((4 * rows, 2 * LANES), BF16), vm((rows, LANES), F32), vm((4 * rows, LANES), F32),
            vm((2 * rows, width), BF16), vm((groups, width + LANES), F32),
            vm((chans, width), BF16), vm((groups, LANES), F32),
            vm((chans, width), F32), vm((rows, chans), F32),
            vm((owners, share, 4, LANES), F32), vm((parts, share, 4, LANES), F32),
            vm((owners, share, LANES), F32), vm((parts, share, LANES), F32),
            vm((parts, share, LANES), F32), vm((owners, share, LANES), F32),
            vm((share, LANES), F32), vm((batch, share, LANES), F32),
            vm((share, LANES), F32), vm((owners, share, LANES), F32),
            pltpu.SemaphoreType.DMA((4,)),
        ] + [pltpu.SemaphoreType.DMA] * 10,
        compiler_params=pltpu.CompilerParams(
            collective_id=0, has_side_effects=True, vmem_limit_bytes=60 * 1024 * 1024
        ),
    )(signal, grad_out, residue, decay)
    return pl.pallas_call(
        finish,
        out_shape=shapes,
        in_specs=[pl.BlockSpec(memory_space=vm)] * 3,
        out_specs=[pl.BlockSpec(memory_space=pl.ANY)] * 3,
        scratch_shapes=[pltpu.SemaphoreType.DMA((3,))],
        compiler_params=pltpu.CompilerParams(vmem_limit_bytes=4 * 1024 * 1024),
    )(*results)


def solution(mesh):
    placed = (P("dp", None, "ctx"), P("dp", None, "ctx"), P(), P())
    return jax.shard_map(
        functools.partial(on_device, mesh.shape["ctx"], mesh.shape["dp"]),
        mesh=mesh,
        in_specs=placed,
        out_specs=(P("dp", None, "ctx"), P(), P()),
        check_vma=False,
    )
```

```python
import functools
import math

import jax
import jax.numpy as jnp
from jax import lax
from jax.experimental import pallas as pl
from jax.experimental.pallas import tpu as pltpu
from jax.sharding import PartitionSpec as P

MESH = pl.DeviceIdType.MESH
F32 = jnp.float32
BF16 = jnp.bfloat16
LANES = 128
OWNERS = 8
HIGH = lax.Precision.HIGHEST


def iota(shape, dim):
    return lax.broadcasted_iota(jnp.int32, shape, dim)


def split(value):
    top = value.astype(BF16)
    return top, (value - top.astype(F32)).astype(BF16)


def wrap(value, size):
    return jnp.where(value >= size, value - size, value)


def down(value, rows):
    return jnp.concatenate([value[rows:], jnp.zeros((rows, value.shape[1]), value.dtype)], axis=0)


def nt(left, right):
    return lax.dot_general(left, right, (((1,), (1,)), ((), ())), preferred_element_type=F32)


def tn(left, right):
    return lax.dot_general(left, right, (((0,), (0,)), ((), ())), preferred_element_type=F32)


def nn(left, right):
    return jnp.dot(left, right, preferred_element_type=F32)


def all_wait(ref, sem):
    pltpu.make_async_copy(ref, ref, sem).wait()


def greet(barrier, axis, me, size):
    for i in range(1, size):
        pl.semaphore_signal(barrier, inc=1, device_id={axis: wrap(me + i, size)}, device_id_type=MESH)


def send(src, dst, send_sem, recv_sem, axis, to):
    pltpu.make_async_remote_copy(
        src_ref=src, dst_ref=dst, send_sem=send_sem, recv_sem=recv_sem, device_id={axis: to}, device_id_type=MESH
    ).start()


def scatter(src_of, dst, send_sem, recv_sem, axis, me, size):
    for i in range(1, size):
        to = wrap(me + i, size)
        send(src_of(to), dst, send_sem, recv_sem, axis, to)


def kernel(
    dims, x_hbm, g_hbm, res_hbm, dec_hbm, outv, pv, qv,
    xv, gv, resv, decv, dcol, rcol, wts, fwd, parts_of, wout, hrow, xrev, lagv, outl, rx,
    send1, recv1, sendl, recvl, send2, recv2, send3, recv3, send4, recv4, spread,
    in_sem, s1, r1, sl, rl, s2, r2, s3, r3, s4, r4,
):
    parts, batch, groups, modes, per_group, width, scale = dims
    rows = groups * modes
    chunks = width // LANES
    me = lax.axis_index("ctx")
    row_of = lax.axis_index("dp")
    owners, share = recv2.shape[0], recv2.shape[1]
    run = owners // 2
    owner_ids = [o // run * (parts // 2) + o % run for o in range(owners)]
    slot = me // (parts // 2) * run + me % (parts // 2)
    is_owner = me % (parts // 2) < run
    plain = jnp.logical_not(is_owner)

    def gather(src, dst, send_sem, recv_sem, some=slice(None)):
        for o, to in list(enumerate(owner_ids))[some]:
            pl.when(me != to)(functools.partial(send, src.at[o], dst.at[me], send_sem, recv_sem, "ctx", to))


    loads = []
    for i, (src, dst) in enumerate(
        [(dec_hbm, decv), (res_hbm, resv)]
        + [
            (src.at[0, pl.ds(h * LANES, LANES)], dst.at[pl.ds(h * LANES, LANES)])
            for h in range(groups * per_group // LANES)
            for src, dst in ((g_hbm, gv), (x_hbm, xv))
        ]
    ):
        loads.append(pltpu.make_async_copy(src, dst, in_sem.at[i]))
        loads[-1].start()
    barrier = pltpu.get_barrier_semaphore()

    @pl.when(is_owner)
    def _():
        greet(barrier, "ctx", me, parts)
        greet(barrier, "dp", row_of, batch)

    eye = iota((modes, modes), 0) == iota((modes, modes), 1)

    def columns(src, dst):
        for g in range(groups):
            column = jnp.sum(jnp.where(eye, src[g : g + 1, :], 0.0), axis=1, keepdims=True)
            dst[g * modes : (g + 1) * modes, :] = jnp.broadcast_to(column, (modes, LANES))

    loads[0].wait()
    dec = decv[...]
    columns(dec, dcol)

    lane = iota((modes, LANES), 1)
    near = lane.astype(F32)
    away = LANES - near
    for g in range(groups):
        at = slice(g * modes, (g + 1) * modes)
        e = jnp.exp(-(dcol[at, :] * near))
        f = jnp.exp(-(dcol[at, :] * away))
        fwd[at, :] = e
        for kind, value in enumerate((e, e * near, f, f * away)):
            r0 = (4 * g + kind) * modes
            wts[r0 : r0 + modes, :LANES], wts[r0 : r0 + modes, LANES:] = split(value)

    def stack(ref, at):
        return jnp.concatenate([ref[at, j * LANES : (j + 1) * LANES] for j in range(chunks)], axis=0)

    segment = iota((8, LANES), 1) // per_group
    own_segment = segment == iota((8, LANES), 0)
    turned_segment = [segment == (iota((8, LANES), 0) + seg) % 8 for seg in range(8)]
    is_grad = lane < chunks * per_group
    steps = jnp.where(is_grad, lane // per_group, 2 * chunks - 1 - lane // per_group).astype(F32) * float(LANES)
    for g in range(groups):
        at = slice(g * modes, (g + 1) * modes)
        chans = slice(g * per_group, (g + 1) * per_group)
        if 2 * g == groups:
            pl.when(is_owner)(lambda: pl.semaphore_wait(barrier, owners - 1 + batch - 1))
            pl.when(plain)(lambda: pl.semaphore_wait(barrier, owners))
            gather(send1, recv1, s1, r1, slice(0, owners // 2))
        if chans.start % LANES == 0:
            for load in loads[2 + 2 * (chans.start // LANES) :][:2]:
                load.wait()
        data = jnp.concatenate([stack(gv, chans), stack(xv, chans)], axis=0)
        o = nt(wts[4 * g * modes : 4 * (g + 1) * modes, :], jnp.concatenate([data, data], axis=1))
        parts_of[4 * g * modes : 4 * (g + 1) * modes, :] = o
        factor = jnp.exp(-(dcol[at, :] * steps))
        gs, gt, xs, xt = (o[kind * modes : (kind + 1) * modes] for kind in range(4))
        for kind, (mask, v) in enumerate(
            ((is_grad, gs), (is_grad, gt + steps * gs), (~is_grad, xs), (~is_grad, xt + steps * xs))
        ):
            v = jnp.where(mask, v * factor, 0.0)
            for shift in (64, 32, 16):
                v = v + pltpu.roll(v, shift, axis=1)
            for h in range(modes // 8):
                k = g * (modes // 8) + h
                seg = g % (LANES // per_group)
                send1[k // share, k % share, kind : kind + 1, :] = jnp.sum(
                    jnp.where(turned_segment[seg], v[h * 8 : (h + 1) * 8], 0.0), axis=0, keepdims=True
                )

    gather(send1, recv1, s1, r1, slice(owners // 2, None))

    anti = (iota((LANES, LANES), 0) + iota((LANES, LANES), 1) == LANES - 1).astype(BF16)
    for i in range(chunks):
        at = slice(i * LANES, (i + 1) * LANES)
        xrev[:, at] = nn(xv[:, at], anti).astype(BF16)
    square_lane = iota((LANES, LANES), 1)
    sub = iota((LANES, LANES), 0)
    wanted = (square_lane < sub) | (square_lane == LANES - 1)
    low = lane % per_group < per_group // 2
    lane_chunk = lane // per_group

    for g in range(groups):
        at = slice(g * per_group, (g + 1) * per_group)
        turned = pltpu.roll(tn(stack(gv, at), stack(xrev, at)), 0, axis=1, stride=1, stride_axis=0)
        lagv[g : g + 1, :] = jnp.sum(jnp.where(wanted, turned, 0.0), axis=0, keepdims=True)
    for g in range(groups):
        at = slice(g * modes, (g + 1) * modes)
        o = parts_of[4 * g * modes : 4 * (g + 1) * modes, :]
        gs, gt = o[:modes], o[modes : 2 * modes]
        xs, xt = (pltpu.roll(o[j * modes : (j + 1) * modes], LANES // 2, axis=1) for j in (2, 3))
        lam = jnp.exp(-(dcol[at, :] * float(LANES)))
        factor, r, rt = 1.0, 0.0, 0.0
        for n in range(1, chunks):
            known = lane_chunk < chunks - n
            a = jnp.where(known, pltpu.roll(gs, LANES - n * per_group, axis=1), 0.0)
            at_n = jnp.where(known, pltpu.roll(gt, LANES - n * per_group, axis=1), 0.0)
            r = r + factor * a
            rt = rt + factor * (at_n + float((n - 1) * LANES) * a)
            factor = factor * lam
        e = fwd[at, :] * pltpu.roll(lagv[g : g + 1, :], 1, axis=1)
        w = e * near + (xs * rt + xt * r)
        e = e + xs * r
        for shift in (64, 32, 16, 8):
            e = e + pltpu.roll(e, shift, axis=1)
            w = w + pltpu.roll(w, shift, axis=1)
        mixed = jnp.where(low, e, w)
        for h in range(modes // 8):
            k = g * (modes // 8) + h
            sendl[k // share, k % share : k % share + 1, :] = jnp.sum(
                jnp.where(own_segment, mixed[h * 8 : (h + 1) * 8], 0.0), axis=0, keepdims=True
            )
    gather(sendl, recvl, sl, rl)

    loads[1].wait()
    series = dec * dec
    series = 1.0 + series / 6.0 * (1.0 + series / 20.0 * (1.0 + series / 42.0 * (1.0 + series / 72.0)))
    norm = jnp.sqrt(2.0 * jnp.exp(-dec) * dec * series)
    columns(resv[...] * norm, rcol)
    later = square_lane >= sub
    back_pos = width - iota((modes, width), 1).astype(F32)

    for g in range(groups):
        at = slice(g * modes, (g + 1) * modes)
        w = jnp.exp(-(jnp.concatenate([dcol[at, :]] * chunks, axis=1) * back_pos))
        w = jnp.concatenate([rcol[at, :]] * chunks, axis=1) * w
        wout[at, :], wout[rows + g * modes : rows + (g + 1) * modes, :] = split(w)
        hrow[g : g + 1, :width] = jnp.sum(w, axis=0, keepdims=True)
        start = jnp.sum(rcol[at, :], axis=0, keepdims=True)
        hrow[g : g + 1, width:] = jnp.where(iota((1, LANES), 1) == 0, start, 0.0)
    for g in range(groups):
        at = slice(g * per_group, (g + 1) * per_group)
        turned = [
            pltpu.roll(
                jnp.broadcast_to(hrow[g : g + 1, b * LANES : (b + 1) * LANES], (LANES, LANES)),
                0, axis=1, stride=1, stride_axis=0,
            )
            for b in range(chunks + 1)
        ]
        blocks = [
            jnp.concatenate(split(jnp.where(later, turned[chunks - b], turned[chunks - 1 - b])), axis=1)
            for b in range(chunks)
        ]
        right = jnp.concatenate(blocks, axis=0)
        left = jnp.concatenate(
            [
                gv[at, :] if i == 0 else jnp.concatenate(
                    [gv[at, i * LANES :], jnp.zeros((per_group, i * LANES), BF16)], axis=1
                )
                for i in range(chunks)
            ],
            axis=0,
        )
        o = nn(left, right)
        o = o[:, :LANES] + o[:, LANES:]
        for i in range(chunks):
            outl[at, i * LANES : (i + 1) * LANES] = o[i * per_group : (i + 1) * per_group, :]
    rx[...] = jnp.zeros_like(rx)

    @pl.when(is_owner)
    def _():
        recv1[pl.ds(me, 1)] = send1[pl.ds(slot, 1)]
        recvl[pl.ds(me, 1)] = sendl[pl.ds(slot, 1)]
        first_half = iota((1, LANES), 1) % per_group < per_group // 2
        factors = []
        for j in range(share):
            k = slot * share + j
            seg = k * 8 // modes % (LANES // per_group)
            mine = dcol[pl.ds(pl.multiple_of(k * 8, 8), 8), :]
            dl = jnp.sum(jnp.where(segment == (iota((8, LANES), 0) + seg) % 8, mine, 0.0), axis=0, keepdims=True)
            factors.append({1 << i: jnp.exp(-(dl * float(width << i))) for i in range(parts.bit_length() - 1)})
        all_wait(recv1.at[pl.ds(0, parts - 1)], r1)
        for j in range(share):
            seg = (slot * share + j) * 8 // modes % (LANES // per_group)
            gs, gt, xs, xt = (recv1[:, j, kind, :] for kind in range(4))
            n = 1
            while n < parts:
                factor = factors[j][n]
                ahead = down(gs, n)
                gt = gt + factor * (down(gt, n) + float(n * width) * ahead)
                gs = gs + factor * ahead
                n *= 2
            gs, gt = down(gs, 1), down(gt, 1)
            send2[:, j, :] = gs
            one = jnp.sum(xs * gs, axis=0, keepdims=True)
            two = jnp.sum(xs * gt + xt * gs, axis=0, keepdims=True)
            one = one + pltpu.roll(one, LANES - per_group // 2, axis=1)
            two = two + pltpu.roll(two, per_group // 2, axis=1)
            send3[j : j + 1, :] = pltpu.roll(jnp.where(first_half, one, two), (8 - seg) % 8 * per_group, axis=1)
        recv2[pl.ds(slot, 1)] = send2[pl.ds(me, 1)]
        all_wait(recvl.at[pl.ds(0, parts - 1)], rl)
        send3[...] = send3[...] + jnp.sum(recvl[...], axis=0)
        recv3[pl.ds(row_of, 1)] = send3[...][None]
        scatter(lambda to: send3, recv3.at[row_of], s3, r3, "dp", row_of, batch)
        scatter(lambda to: send2.at[to], recv2.at[slot], s2, r2, "ctx", me, parts)
        all_wait(recv3.at[pl.ds(0, batch - 1)], r3)
        total = recv3[0]
        for b in range(1, batch):
            total = total + recv3[b]
        send4[...] = total
        recv4[pl.ds(slot, 1)] = total[None]
        scatter(lambda to: send4, recv4.at[slot], s4, r4, "ctx", me, parts)
        all_wait(recv2.at[pl.ds(0, owners - 1)], r2)

    pl.when(plain)(lambda: all_wait(recv2, r2))

    for k in range(parts):
        first = (k * 8 // modes) * per_group
        half, seg = first // LANES, (first % LANES) // per_group
        v = jnp.broadcast_to(recv2[k // share, k % share : k % share + 1, :], (8, LANES))
        v = jnp.where(turned_segment[seg], v, 0.0)
        for shift in (64, 32, 16):
            v = v + pltpu.roll(v, shift, axis=1)
        v = jnp.where(segment == seg, v, 0.0)
        rx[k * 8 : (k + 1) * 8, half * LANES : (half + 1) * LANES] = v
    r_top, r_low = split(rx[...])
    w_top, w_low = wout[:rows, :], wout[rows:, :]
    far = tn(jnp.concatenate([r_top, r_top, r_low], axis=0), jnp.concatenate([w_top, w_low, w_top], axis=0))
    outv[0] = (outl[...] + far).astype(BF16)

    from_lane, to_lane = iota((LANES, LANES), 0), iota((LANES, LANES), 1)
    same_mode = from_lane // per_group == to_lane % 8
    kind_of = (from_lane % per_group >= per_group // 2) == (to_lane >= LANES // 2)
    select = jnp.where(same_mode & kind_of & (to_lane % (LANES // 2) < modes), 1.0, 0.0)
    pl.when(is_owner)(lambda: all_wait(recv4.at[pl.ds(0, owners - 1)], r4))
    pl.when(plain)(lambda: all_wait(recv4, r4))
    sums = jnp.concatenate([recv4[o] for o in range(owners)], axis=0)
    sums = jnp.dot(sums, select, precision=HIGH, preferred_element_type=F32)
    sums = jnp.where(iota((parts, LANES), 0) % 2 == iota((parts, LANES), 1) % modes // 8, sums, 0.0)
    spread[...] = sums
    total = spread[pl.ds(0, groups, stride=2), :] + spread[pl.ds(1, groups, stride=2), :]
    pv[...] = total[:, :modes] * (norm * scale)
    qv[...] = total[:, LANES // 2 : LANES // 2 + modes] * (dec * norm * scale)

    @pl.when(is_owner)
    def _():
        all_wait(send1.at[pl.ds(0, owners - 1)], s1)
        all_wait(sendl.at[pl.ds(0, owners - 1)], sl)
        all_wait(send2.at[pl.ds(0, parts - 1)], s2)
        all_wait(recv3.at[pl.ds(0, batch - 1)], s3)
        all_wait(recvl.at[pl.ds(0, parts - 1)], s4)

    @pl.when(plain)
    def _():
        all_wait(send1, s1)
        all_wait(sendl, sl)


def finish(*refs):
    copies = [pltpu.make_async_copy(refs[i], refs[3 + i], refs[6].at[i]) for i in range(3)]
    for copy in copies:
        copy.start()
    for copy in copies:
        copy.wait()


def on_device(parts, batch, signal, grad_out, residue, decay):
    _, chans, width = signal.shape
    groups, modes = residue.shape
    per_group = chans // groups
    rows = groups * modes
    scale = 1.0 / math.sqrt(per_group * batch * parts * width)
    owners = OWNERS
    share = rows // 8 // owners
    dims = (parts, batch, groups, modes, per_group, width, scale)
    vm = pltpu.VMEM
    shapes = (
        jax.ShapeDtypeStruct(signal.shape, BF16),
        jax.ShapeDtypeStruct((groups, modes), F32),
        jax.ShapeDtypeStruct((groups, modes), F32),
    )
    results = pl.pallas_call(
        functools.partial(kernel, dims),
        out_shape=tuple(vm(shape.shape, shape.dtype) for shape in shapes),
        in_specs=[pl.BlockSpec(memory_space=pl.ANY)] * 4,
        out_specs=[pl.BlockSpec(memory_space=vm)] * 3,
        scratch_shapes=[
            vm((chans, width), BF16), vm((chans, width), BF16), vm((groups, modes), F32), vm((groups, modes), F32),
            vm((rows, LANES), F32), vm((rows, LANES), F32),
            vm((4 * rows, 2 * LANES), BF16), vm((rows, LANES), F32), vm((4 * rows, LANES), F32),
            vm((2 * rows, width), BF16), vm((groups, width + LANES), F32),
            vm((chans, width), BF16), vm((groups, LANES), F32),
            vm((chans, width), F32), vm((rows, chans), F32),
            vm((owners, share, 4, LANES), F32), vm((parts, share, 4, LANES), F32),
            vm((owners, share, LANES), F32), vm((parts, share, LANES), F32),
            vm((parts, share, LANES), F32), vm((owners, share, LANES), F32),
            vm((share, LANES), F32), vm((batch, share, LANES), F32),
            vm((share, LANES), F32), vm((owners, share, LANES), F32), vm((rows // 8, LANES), F32),
            pltpu.SemaphoreType.DMA((2 + 2 * (chans // LANES),)),
        ] + [pltpu.SemaphoreType.DMA] * 10,
        compiler_params=pltpu.CompilerParams(
            collective_id=0, has_side_effects=True, vmem_limit_bytes=60 * 1024 * 1024
        ),
    )(signal, grad_out, residue, decay)
    return pl.pallas_call(
        finish,
        out_shape=shapes,
        in_specs=[pl.BlockSpec(memory_space=vm)] * 3,
        out_specs=[pl.BlockSpec(memory_space=pl.ANY)] * 3,
        scratch_shapes=[pltpu.SemaphoreType.DMA((3,))],
        compiler_params=pltpu.CompilerParams(vmem_limit_bytes=4 * 1024 * 1024),
    )(*results)


def solution(mesh):
    placed = (P("dp", None, "ctx"), P("dp", None, "ctx"), P(), P())
    return jax.shard_map(
        functools.partial(on_device, mesh.shape["ctx"], mesh.shape["dp"]),
        mesh=mesh,
        in_specs=placed,
        out_specs=(P("dp", None, "ctx"), P(), P()),
        check_vma=False,
    )
```

```python
import functools
import math

import jax
import jax.numpy as jnp
from jax import lax
from jax.experimental import pallas as pl
from jax.experimental.pallas import tpu as pltpu
from jax.sharding import PartitionSpec as P

MESH = pl.DeviceIdType.MESH
F32 = jnp.float32
BF16 = jnp.bfloat16
LANES = 128
OWNERS = 8


def iota(shape, dim):
    return lax.broadcasted_iota(jnp.int32, shape, dim)


def split(value):
    top = value.astype(BF16)
    return top, (value - top.astype(F32)).astype(BF16)


def wrap(value, size):
    return jnp.where(value >= size, value - size, value)


def down(value, rows):
    return jnp.concatenate([value[rows:], jnp.zeros((rows, value.shape[1]), value.dtype)], axis=0)


def nt(left, right):
    return lax.dot_general(left, right, (((1,), (1,)), ((), ())), preferred_element_type=F32)


def tn(left, right):
    return lax.dot_general(left, right, (((0,), (0,)), ((), ())), preferred_element_type=F32)


def nn(left, right):
    return jnp.dot(left, right, preferred_element_type=F32)


def all_wait(ref, sem):
    pltpu.make_async_copy(ref, ref, sem).wait()


def greet(barrier, axis, me, size):
    for i in range(1, size):
        pl.semaphore_signal(barrier, inc=1, device_id={axis: wrap(me + i, size)}, device_id_type=MESH)


def send(src, dst, send_sem, recv_sem, axis, to):
    pltpu.make_async_remote_copy(
        src_ref=src, dst_ref=dst, send_sem=send_sem, recv_sem=recv_sem, device_id={axis: to}, device_id_type=MESH
    ).start()


def scatter(src_of, dst, send_sem, recv_sem, axis, me, size):
    for i in range(1, size):
        to = wrap(me + i, size)
        send(src_of(to), dst, send_sem, recv_sem, axis, to)


def kernel(
    dims, x_hbm, g_hbm, res_hbm, dec_hbm, outv, pv, qv,
    xv, gv, resv, decv, dcol, rcol, wts, fwd, parts_of, wout, hrow, xrev, lagv, outl, rx,
    send1, recv1, sendl, recvl, send2, recv2, send3, recv3, send4, recv4, spread,
    in_sem, s1, r1, sl, rl, s2, r2, s3, r3, s4, r4,
):
    parts, batch, groups, modes, per_group, width, scale = dims
    rows = groups * modes
    chunks = width // LANES
    me = lax.axis_index("ctx")
    row_of = lax.axis_index("dp")
    owners, share = recv2.shape[0], recv2.shape[1]
    run = owners // 2
    owner_ids = [o // run * (parts // 2) + o % run for o in range(owners)]
    slot = me // (parts // 2) * run + me % (parts // 2)
    is_owner = me % (parts // 2) < run
    plain = jnp.logical_not(is_owner)

    def gather(src, dst, send_sem, recv_sem, some=slice(None)):
        for o, to in list(enumerate(owner_ids))[some]:
            pl.when(me != to)(functools.partial(send, src.at[o], dst.at[me], send_sem, recv_sem, "ctx", to))


    loads = []
    for i, (src, dst) in enumerate(
        [(dec_hbm, decv), (res_hbm, resv)]
        + [
            (src.at[0, pl.ds(h * LANES, LANES)], dst.at[pl.ds(h * LANES, LANES)])
            for h in range(groups * per_group // LANES)
            for src, dst in ((g_hbm, gv), (x_hbm, xv))
        ]
    ):
        loads.append(pltpu.make_async_copy(src, dst, in_sem.at[i]))
        loads[-1].start()
    barrier = pltpu.get_barrier_semaphore()

    @pl.when(is_owner)
    def _():
        greet(barrier, "ctx", me, parts)
        greet(barrier, "dp", row_of, batch)

    eye = iota((modes, modes), 0) == iota((modes, modes), 1)

    def columns(src, dst):
        for g in range(groups):
            column = jnp.sum(jnp.where(eye, src[g : g + 1, :], 0.0), axis=1, keepdims=True)
            dst[g * modes : (g + 1) * modes, :] = jnp.broadcast_to(column, (modes, LANES))

    loads[0].wait()
    dec = decv[...]
    columns(dec, dcol)

    lane = iota((modes, LANES), 1)
    near = lane.astype(F32)
    away = LANES - near
    for g in range(groups):
        at = slice(g * modes, (g + 1) * modes)
        e = jnp.exp(-(dcol[at, :] * near))
        f = jnp.exp(-(dcol[at, :] * away))
        fwd[at, :] = e
        for kind, value in enumerate((e, e * near, f, f * away)):
            r0 = (4 * g + kind) * modes
            wts[r0 : r0 + modes, :LANES], wts[r0 : r0 + modes, LANES:] = split(value)

    def stack(ref, at):
        return jnp.concatenate([ref[at, j * LANES : (j + 1) * LANES] for j in range(chunks)], axis=0)

    segment = iota((8, LANES), 1) // per_group
    own_segment = segment == iota((8, LANES), 0)
    turned_segment = [segment == (iota((8, LANES), 0) + seg) % 8 for seg in range(8)]
    is_grad = lane < chunks * per_group
    steps = jnp.where(is_grad, lane // per_group, 2 * chunks - 1 - lane // per_group).astype(F32) * float(LANES)
    for g in range(groups):
        at = slice(g * modes, (g + 1) * modes)
        chans = slice(g * per_group, (g + 1) * per_group)
        if 2 * g == groups:
            pl.when(is_owner)(lambda: pl.semaphore_wait(barrier, owners - 1 + batch - 1))
            pl.when(plain)(lambda: pl.semaphore_wait(barrier, owners))
            gather(send1, recv1, s1, r1, slice(0, owners // 2))
        if chans.start % LANES == 0:
            for load in loads[2 + 2 * (chans.start // LANES) :][:2]:
                load.wait()
        data = jnp.concatenate([stack(gv, chans), stack(xv, chans)], axis=0)
        o = nt(wts[4 * g * modes : 4 * (g + 1) * modes, :], jnp.concatenate([data, data], axis=1))
        parts_of[4 * g * modes : 4 * (g + 1) * modes, :] = o
        factor = jnp.exp(-(dcol[at, :] * steps))
        gs, gt, xs, xt = (o[kind * modes : (kind + 1) * modes] for kind in range(4))
        for kind, (mask, v) in enumerate(
            ((is_grad, gs), (is_grad, gt + steps * gs), (~is_grad, xs), (~is_grad, xt + steps * xs))
        ):
            v = jnp.where(mask, v * factor, 0.0)
            for shift in (64, 32, 16):
                v = v + pltpu.roll(v, shift, axis=1)
            for h in range(modes // 8):
                k = g * (modes // 8) + h
                seg = g % (LANES // per_group)
                send1[k // share, k % share, kind : kind + 1, :] = jnp.sum(
                    jnp.where(turned_segment[seg], v[h * 8 : (h + 1) * 8], 0.0), axis=0, keepdims=True
                )

    gather(send1, recv1, s1, r1, slice(owners // 2, None))

    anti = (iota((LANES, LANES), 0) + iota((LANES, LANES), 1) == LANES - 1).astype(BF16)
    for i in range(chunks):
        at = slice(i * LANES, (i + 1) * LANES)
        xrev[:, at] = nn(xv[:, at], anti).astype(BF16)
    square_lane = iota((LANES, LANES), 1)
    sub = iota((LANES, LANES), 0)
    wanted = (square_lane < sub) | (square_lane == LANES - 1)
    low = lane % per_group < per_group // 2
    lane_chunk = lane // per_group

    for g in range(groups):
        at = slice(g * per_group, (g + 1) * per_group)
        turned = pltpu.roll(tn(stack(gv, at), stack(xrev, at)), 0, axis=1, stride=1, stride_axis=0)
        lagv[g : g + 1, :] = jnp.sum(jnp.where(wanted, turned, 0.0), axis=0, keepdims=True)
    for g in range(groups):
        at = slice(g * modes, (g + 1) * modes)
        o = parts_of[4 * g * modes : 4 * (g + 1) * modes, :]
        gs, gt = o[:modes], o[modes : 2 * modes]
        xs, xt = (pltpu.roll(o[j * modes : (j + 1) * modes], LANES // 2, axis=1) for j in (2, 3))
        lam = jnp.exp(-(dcol[at, :] * float(LANES)))
        factor, r, rt = 1.0, 0.0, 0.0
        for n in range(1, chunks):
            known = lane_chunk < chunks - n
            a = jnp.where(known, pltpu.roll(gs, LANES - n * per_group, axis=1), 0.0)
            at_n = jnp.where(known, pltpu.roll(gt, LANES - n * per_group, axis=1), 0.0)
            r = r + factor * a
            rt = rt + factor * (at_n + float((n - 1) * LANES) * a)
            factor = factor * lam
        e = fwd[at, :] * pltpu.roll(lagv[g : g + 1, :], 1, axis=1)
        w = e * near + (xs * rt + xt * r)
        e = e + xs * r
        for shift in (64, 32, 16, 8):
            e = e + pltpu.roll(e, shift, axis=1)
            w = w + pltpu.roll(w, shift, axis=1)
        mixed = jnp.where(low, e, w)
        for h in range(modes // 8):
            k = g * (modes // 8) + h
            sendl[k // share, k % share : k % share + 1, :] = jnp.sum(
                jnp.where(own_segment, mixed[h * 8 : (h + 1) * 8], 0.0), axis=0, keepdims=True
            )
    gather(sendl, recvl, sl, rl)

    loads[1].wait()
    series = dec * dec
    series = 1.0 + series / 6.0 * (1.0 + series / 20.0 * (1.0 + series / 42.0 * (1.0 + series / 72.0)))
    norm = jnp.sqrt(2.0 * jnp.exp(-dec) * dec * series)
    columns(resv[...] * norm, rcol)
    later = square_lane >= sub
    back_pos = width - iota((modes, width), 1).astype(F32)

    for g in range(groups):
        at = slice(g * modes, (g + 1) * modes)
        w = jnp.exp(-(jnp.concatenate([dcol[at, :]] * chunks, axis=1) * back_pos))
        w = jnp.concatenate([rcol[at, :]] * chunks, axis=1) * w
        wout[at, :], wout[rows + g * modes : rows + (g + 1) * modes, :] = split(w)
        hrow[g : g + 1, :width] = jnp.sum(w, axis=0, keepdims=True)
        start = jnp.sum(rcol[at, :], axis=0, keepdims=True)
        hrow[g : g + 1, width:] = jnp.where(iota((1, LANES), 1) == 0, start, 0.0)
    for g in range(groups):
        at = slice(g * per_group, (g + 1) * per_group)
        turned = [
            pltpu.roll(
                jnp.broadcast_to(hrow[g : g + 1, b * LANES : (b + 1) * LANES], (LANES, LANES)),
                0, axis=1, stride=1, stride_axis=0,
            )
            for b in range(chunks + 1)
        ]
        blocks = [
            jnp.concatenate(split(jnp.where(later, turned[chunks - b], turned[chunks - 1 - b])), axis=1)
            for b in range(chunks)
        ]
        right = jnp.concatenate(blocks, axis=0)
        left = jnp.concatenate(
            [
                gv[at, :] if i == 0 else jnp.concatenate(
                    [gv[at, i * LANES :], jnp.zeros((per_group, i * LANES), BF16)], axis=1
                )
                for i in range(chunks)
            ],
            axis=0,
        )
        o = nn(left, right)
        o = o[:, :LANES] + o[:, LANES:]
        for i in range(chunks):
            outl[at, i * LANES : (i + 1) * LANES] = o[i * per_group : (i + 1) * per_group, :]
    rx[...] = jnp.zeros_like(rx)

    @pl.when(is_owner)
    def _():
        recv1[pl.ds(me, 1)] = send1[pl.ds(slot, 1)]
        recvl[pl.ds(me, 1)] = sendl[pl.ds(slot, 1)]
        first_half = iota((1, LANES), 1) % per_group < per_group // 2
        factors = []
        for j in range(share):
            k = slot * share + j
            seg = k * 8 // modes % (LANES // per_group)
            mine = dcol[pl.ds(pl.multiple_of(k * 8, 8), 8), :]
            dl = jnp.sum(jnp.where(segment == (iota((8, LANES), 0) + seg) % 8, mine, 0.0), axis=0, keepdims=True)
            factors.append({1 << i: jnp.exp(-(dl * float(width << i))) for i in range(parts.bit_length() - 1)})
        all_wait(recv1.at[pl.ds(0, parts - 1)], r1)
        for j in range(share):
            seg = (slot * share + j) * 8 // modes % (LANES // per_group)
            gs, gt, xs, xt = (recv1[:, j, kind, :] for kind in range(4))
            n = 1
            while n < parts:
                factor = factors[j][n]
                ahead = down(gs, n)
                gt = gt + factor * (down(gt, n) + float(n * width) * ahead)
                gs = gs + factor * ahead
                n *= 2
            gs, gt = down(gs, 1), down(gt, 1)
            send2[:, j, :] = gs
            one = jnp.sum(xs * gs, axis=0, keepdims=True)
            two = jnp.sum(xs * gt + xt * gs, axis=0, keepdims=True)
            one = one + pltpu.roll(one, LANES - per_group // 2, axis=1)
            two = two + pltpu.roll(two, per_group // 2, axis=1)
            send3[j : j + 1, :] = pltpu.roll(jnp.where(first_half, one, two), (8 - seg) % 8 * per_group, axis=1)
        recv2[pl.ds(slot, 1)] = send2[pl.ds(me, 1)]
        all_wait(recvl.at[pl.ds(0, parts - 1)], rl)
        send3[...] = send3[...] + jnp.sum(recvl[...], axis=0)
        recv3[pl.ds(row_of, 1)] = send3[...][None]
        scatter(lambda to: send3, recv3.at[row_of], s3, r3, "dp", row_of, batch)
        scatter(lambda to: send2.at[to], recv2.at[slot], s2, r2, "ctx", me, parts)
        all_wait(recv3.at[pl.ds(0, batch - 1)], r3)
        total = recv3[0]
        for b in range(1, batch):
            total = total + recv3[b]
        send4[...] = total
        recv4[pl.ds(slot, 1)] = total[None]
        scatter(lambda to: send4, recv4.at[slot], s4, r4, "ctx", me, parts)
        all_wait(recv2.at[pl.ds(0, owners - 1)], r2)

    pl.when(plain)(lambda: all_wait(recv2, r2))

    for k in range(parts):
        first = (k * 8 // modes) * per_group
        half, seg = first // LANES, (first % LANES) // per_group
        v = jnp.broadcast_to(recv2[k // share, k % share : k % share + 1, :], (8, LANES))
        v = jnp.where(turned_segment[seg], v, 0.0)
        for shift in (64, 32, 16):
            v = v + pltpu.roll(v, shift, axis=1)
        v = jnp.where(segment == seg, v, 0.0)
        rx[k * 8 : (k + 1) * 8, half * LANES : (half + 1) * LANES] = v
    r_top, r_low = split(rx[...])
    w_top, w_low = wout[:rows, :], wout[rows:, :]
    far = tn(jnp.concatenate([r_top, r_top, r_low], axis=0), jnp.concatenate([w_top, w_low, w_top], axis=0))
    outv[0] = (outl[...] + far).astype(BF16)

    from_lane, to_lane = iota((LANES, LANES), 0), iota((LANES, LANES), 1)
    same_mode = from_lane // per_group == to_lane % 8
    kind_of = (from_lane % per_group >= per_group // 2) == (to_lane >= LANES // 2)
    select = jnp.where(same_mode & kind_of & (to_lane % (LANES // 2) < modes), 1.0, 0.0)
    pl.when(is_owner)(lambda: all_wait(recv4.at[pl.ds(0, owners - 1)], r4))
    pl.when(plain)(lambda: all_wait(recv4, r4))
    sums = jnp.concatenate([recv4[o] for o in range(owners)], axis=0)
    select = select.astype(BF16)
    sums = nn(jnp.concatenate(split(sums), axis=1), jnp.concatenate([select, select], axis=0))
    sums = jnp.where(iota((parts, LANES), 0) % 2 == iota((parts, LANES), 1) % modes // 8, sums, 0.0)
    spread[...] = sums
    total = spread[pl.ds(0, groups, stride=2), :] + spread[pl.ds(1, groups, stride=2), :]
    pv[...] = total[:, :modes] * (norm * scale)
    qv[...] = total[:, LANES // 2 : LANES // 2 + modes] * (dec * norm * scale)

    @pl.when(is_owner)
    def _():
        all_wait(send1.at[pl.ds(0, owners - 1)], s1)
        all_wait(sendl.at[pl.ds(0, owners - 1)], sl)
        all_wait(send2.at[pl.ds(0, parts - 1)], s2)
        all_wait(recv3.at[pl.ds(0, batch - 1)], s3)
        all_wait(recvl.at[pl.ds(0, parts - 1)], s4)

    @pl.when(plain)
    def _():
        all_wait(send1, s1)
        all_wait(sendl, sl)


def finish(*refs):
    copies = [pltpu.make_async_copy(refs[i], refs[3 + i], refs[6].at[i]) for i in range(3)]
    for copy in copies:
        copy.start()
    for copy in copies:
        copy.wait()


def on_device(parts, batch, signal, grad_out, residue, decay):
    _, chans, width = signal.shape
    groups, modes = residue.shape
    per_group = chans // groups
    rows = groups * modes
    scale = 1.0 / math.sqrt(per_group * batch * parts * width)
    owners = OWNERS
    share = rows // 8 // owners
    dims = (parts, batch, groups, modes, per_group, width, scale)
    vm = pltpu.VMEM
    shapes = (
        jax.ShapeDtypeStruct(signal.shape, BF16),
        jax.ShapeDtypeStruct((groups, modes), F32),
        jax.ShapeDtypeStruct((groups, modes), F32),
    )
    results = pl.pallas_call(
        functools.partial(kernel, dims),
        out_shape=tuple(vm(shape.shape, shape.dtype) for shape in shapes),
        in_specs=[pl.BlockSpec(memory_space=pl.ANY)] * 4,
        out_specs=[pl.BlockSpec(memory_space=vm)] * 3,
        scratch_shapes=[
            vm((chans, width), BF16), vm((chans, width), BF16), vm((groups, modes), F32), vm((groups, modes), F32),
            vm((rows, LANES), F32), vm((rows, LANES), F32),
            vm((4 * rows, 2 * LANES), BF16), vm((rows, LANES), F32), vm((4 * rows, LANES), F32),
            vm((2 * rows, width), BF16), vm((groups, width + LANES), F32),
            vm((chans, width), BF16), vm((groups, LANES), F32),
            vm((chans, width), F32), vm((rows, chans), F32),
            vm((owners, share, 4, LANES), F32), vm((parts, share, 4, LANES), F32),
            vm((owners, share, LANES), F32), vm((parts, share, LANES), F32),
            vm((parts, share, LANES), F32), vm((owners, share, LANES), F32),
            vm((share, LANES), F32), vm((batch, share, LANES), F32),
            vm((share, LANES), F32), vm((owners, share, LANES), F32), vm((rows // 8, LANES), F32),
            pltpu.SemaphoreType.DMA((2 + 2 * (chans // LANES),)),
        ] + [pltpu.SemaphoreType.DMA] * 10,
        compiler_params=pltpu.CompilerParams(
            collective_id=0, has_side_effects=True, vmem_limit_bytes=60 * 1024 * 1024
        ),
    )(signal, grad_out, residue, decay)
    return pl.pallas_call(
        finish,
        out_shape=shapes,
        in_specs=[pl.BlockSpec(memory_space=vm)] * 3,
        out_specs=[pl.BlockSpec(memory_space=pl.ANY)] * 3,
        scratch_shapes=[pltpu.SemaphoreType.DMA((3,))],
        compiler_params=pltpu.CompilerParams(vmem_limit_bytes=4 * 1024 * 1024),
    )(*results)


def solution(mesh):
    placed = (P("dp", None, "ctx"), P("dp", None, "ctx"), P(), P())
    return jax.shard_map(
        functools.partial(on_device, mesh.shape["ctx"], mesh.shape["dp"]),
        mesh=mesh,
        in_specs=placed,
        out_specs=(P("dp", None, "ctx"), P(), P()),
        check_vma=False,
    )
```
